512 devices in a mesh: row: 64 (over y_hi, z, core), col: 8 (over x, y_lo).
Axes of the slice: x: 4, y: 8 (y_hi: 4, y_lo: 2; y = y_hi * 2 + y_lo), z: 8, core: 2. Of those that a mesh axis runs over, the one named last changes fastest.
Arguments:
- dens_a: bfloat16 [64, 8, 1, 3, 256, 256], P('row', 'col')
- dens_b: bfloat16 [64, 8, 1, 3, 256, 256], P('row', 'col')
- codes_a: int32 [64, 8, 1, 3], P('row', 'col'), may hold values from 0 to 4, as said below
- codes_b: int32 [64, 8, 1, 3], P('row', 'col'), may hold values from 0 to 4, as said below
- counts_a: int32 [64, 8, 1], P('row', 'col'), may hold values from 1 to 3
- counts_b: int32 [64, 8, 1], P('row', 'col'), may hold values from 1 to 3
Outputs:
- new_a: bfloat16 [64, 8, 1, 3, 256, 256], P('row', 'col')
- new_b: bfloat16 [64, 8, 1, 3, 256, 256], P('row', 'col')
The draws below stay inside these ranges and needn't reach their ends.
Inputs may be any that keep to these rules, and one draw needn't show every extreme that they name: `codes_a`: within a block row the codes of all slots are distinct. `codes_b`: within a block row the codes of all slots are distinct.
All inputs are finite; a program needn't handle non-finite values.
Results may differ from the reference program's by a relative error of at most 0.0092.
Values may be sent and summed in bfloat16 or wider, within the bound.
A program may use at most 64 MiB of HBM per device.

```python
import jax
import jax.numpy as jnp
from jax import lax

BLOCK = 256
ROWS_DEV = 1
TILES = 3
ITERS = 2
N_ROW = 64
N_COL = 8


def occupations(key):
    shape = (N_ROW, N_COL, ROWS_DEV, 1, 1, BLOCK)
    side = jax.random.randint(jax.random.fold_in(key, 2), shape, 0, 2).astype(jnp.float32)
    level = jax.random.uniform(jax.random.fold_in(key, 3), shape, minval=0.05, maxval=0.2)
    return level + 0.75 * side


def with_diagonal(noise, occupancy):
    identity = jnp.eye(BLOCK, dtype=jnp.float32)
    leading = (jnp.arange(TILES) == 0).astype(jnp.float32)
    return (noise + leading[:, None, None] * identity * occupancy).astype(jnp.bfloat16)


def density_draw(key):
    shape = (N_ROW, N_COL, ROWS_DEV, TILES, BLOCK, BLOCK)
    occupancy = occupations(jax.random.fold_in(key, 5))
    noise = 0.02 * jax.random.normal(key, shape)
    return with_diagonal(noise, occupancy)


def pattern_codes(key):
    span = 5 * ROWS_DEV
    shape = (N_ROW, N_COL, ROWS_DEV, span)
    scores = jax.random.randint(key, shape, 0, 1 << 16) * span + jnp.arange(span, dtype=jnp.int32)
    itself = jnp.arange(ROWS_DEV, dtype=jnp.int32)[:, None] == jnp.arange(span, dtype=jnp.int32)[None, :]
    scores = jnp.where(itself, -1, scores)
    return jnp.argsort(scores, axis=-1)[..., :TILES].astype(jnp.int32)


def pattern_counts(key):
    counts = jax.random.randint(key, (N_ROW, N_COL, ROWS_DEV), 1, TILES + 1)
    counts = counts.at[0, 0, 0].set(TILES)
    counts = counts.at[N_ROW - 1, N_COL - 1, ROWS_DEV - 1].set(1)
    return counts.astype(jnp.int32)


def draw_dens_a(key, part):
    key = jax.random.fold_in(key, 11)
    return density_draw(key)


def draw_dens_b(key, part):
    key = jax.random.fold_in(key, 12)
    return density_draw(key)


def draw_codes_a(key, part):
    key = jax.random.fold_in(key, 13)
    return pattern_codes(key)


def draw_codes_b(key, part):
    key = jax.random.fold_in(key, 14)
    return pattern_codes(key)


def draw_counts_a(key, part):
    key = jax.random.fold_in(key, 15)
    return pattern_counts(key)


def draw_counts_b(key, part):
    key = jax.random.fold_in(key, 16)
    return pattern_counts(key)


def setup_inputs(seed: int = 0) -> dict:
    splits = jax.random.split(jax.random.key(seed), 7)
    dens_a = draw_dens_a(jax.random.fold_in(splits[6], 71), 0)
    dens_b = draw_dens_b(jax.random.fold_in(splits[6], 71), 0)
    codes_a = draw_codes_a(jax.random.fold_in(splits[6], 71), 0)
    codes_b = draw_codes_b(jax.random.fold_in(splits[6], 71), 0)
    counts_a = draw_counts_a(jax.random.fold_in(splits[6], 71), 0)
    counts_b = draw_counts_b(jax.random.fold_in(splits[6], 71), 0)
    return dict(dens_a=dens_a, dens_b=dens_b, codes_a=codes_a, codes_b=codes_b, counts_a=counts_a, counts_b=counts_b)


def displacement(direction):
    vertical = (direction == 2).astype(jnp.int32) - (direction == 1).astype(jnp.int32)
    lateral = (direction == 4).astype(jnp.int32) - (direction == 3).astype(jnp.int32)
    return vertical, lateral


def purify_region(tiles, codes, counts):
    rows = tiles.shape[1]
    slots = tiles.shape[2]
    edge = tiles.shape[3]
    flat_tiles = tiles.reshape(5 * rows, slots, edge, edge)
    flat_codes = codes.reshape(5 * rows, slots)
    flat_counts = counts.reshape(5 * rows)
    own_codes = codes[0]
    order = jnp.arange(slots, dtype=jnp.int32)
    own_live = order[None, :] < counts[0][:, None]
    partner = jnp.take(flat_tiles, own_codes, axis=0)
    partner_codes = jnp.take(flat_codes, own_codes, axis=0)
    partner_live = order[None, None, :] < jnp.take(flat_counts, own_codes, axis=0)[:, :, None]
    first_vert, first_side = displacement(own_codes // rows)
    second_vert, second_side = displacement(partner_codes // rows)
    matches = own_live[:, :, None, None] & partner_live[:, :, :, None] & own_live[:, None, None, :]
    matches = matches & (first_vert[:, :, None, None] + second_vert[:, :, :, None] == first_vert[:, None, None, :])
    matches = matches & (first_side[:, :, None, None] + second_side[:, :, :, None] == first_side[:, None, None, :])
    matches = matches & (partner_codes[:, :, :, None] % rows == own_codes[:, None, None, :] % rows)
    chosen = jnp.einsum("qabs,qabxy->qasxy", matches.astype(jnp.float32), partner.astype(jnp.float32))
    square = jnp.einsum("qaxy,qasyz->qsxz", tiles[0].astype(jnp.float32), chosen)
    square_low = lax.optimization_barrier(square.astype(jnp.bfloat16))
    square_back = square_low.astype(jnp.float32)
    cube = jnp.einsum("qaxy,qasyz->qsxz", square_back, chosen)
    return (3.0 * square_back - 2.0 * cube).astype(jnp.bfloat16)


def one_step(dens, codes, counts):
    grid_rows = dens.shape[0]
    grid_cols = dens.shape[1]

    def region(index):
        here_row = index // grid_cols
        here_col = index % grid_cols
        upper = (here_row - 1) % grid_rows
        lower = (here_row + 1) % grid_rows
        left_col = (here_col - 1) % grid_cols
        right_col = (here_col + 1) % grid_cols
        row_pick = jnp.stack([here_row, upper, lower, here_row, here_row]).astype(jnp.int32)
        col_pick = jnp.stack([here_col, here_col, here_col, left_col, right_col]).astype(jnp.int32)
        return purify_region(dens[row_pick, col_pick], codes[row_pick, col_pick], counts[row_pick, col_pick])

    result = lax.map(region, jnp.arange(grid_rows * grid_cols, dtype=jnp.int32))
    return result.reshape(dens.shape)


def advance(dens, codes, counts):
    for step in range(ITERS):
        dens = one_step(dens, codes, counts)
    return dens


def reference(dens_a, dens_b, codes_a, codes_b, counts_a, counts_b):
    return advance(dens_a, codes_a, counts_a), advance(dens_b, codes_b, counts_b)
```

```python
import jax
import jax.numpy as jnp
from jax import lax
from jax.experimental import pallas as pl
from jax.experimental.pallas import tpu as pltpu
from jax.sharding import PartitionSpec as P

OUT_X, DIAG, OUT_Z, IN_X, IN_Z, NONE = range(6)
BESIDE = (OUT_X, OUT_Z, IN_X, IN_Z)
MESH = pl.DeviceIdType.MESH
EDGE = 256
SLOTS = 3
HELD = 16


def beside(name):
    return NONE + 1 + 2 * name


def names_of(codes_ref, count_ref, row_bit, col_bit):
    names = []
    for slot in range(SLOTS):
        code = codes_ref[slot]
        vertical = jnp.where(code - 1 == row_bit, OUT_Z, IN_Z)
        lateral = jnp.where(code - 3 == col_bit, OUT_X, IN_X)
        name = jnp.where(code == 0, DIAG, jnp.where(code <= 2, vertical, lateral))
        names.append(jnp.where(slot < count_ref[0], name, NONE))
    return names


def in_order(names):
    a, b, c = (names[slot] * 4 + slot for slot in range(SLOTS))
    a, b = jnp.minimum(a, b), jnp.maximum(a, b)
    b, c = jnp.minimum(b, c), jnp.maximum(b, c)
    a, b = jnp.minimum(a, b), jnp.maximum(a, b)
    return [v // 4 for v in (a, b, c)], [v % 4 for v in (a, b, c)]


def diagonal_first(order):
    first, second, third = order
    has = (first == DIAG) | (second == DIAG)
    return [jnp.where(has, DIAG, first), jnp.where(second == DIAG, first, second), third], has


def place(names, wanted):
    at = jnp.int32(SLOTS)
    for index in reversed(range(SLOTS)):
        at = jnp.where(names[index] == wanted, index, at)
    return at


def matmul(x, y):
    return jnp.dot(x, y, preferred_element_type=jnp.float32)


def kernel(
    dens_a, dens_b, codes_a, codes_b, count_a, count_b, out_a, out_b,
    loaded, swap_out, swap_in, meta_out, meta_in, *rest,
):
    held = {(step, region): rest[2 * step + region] for step in (0, 1) for region in (0, 1)}
    fresh = {(step, region): rest[4 + 2 * step + region] for step in (0, 1) for region in (0, 1)}
    back, load_sem, swap_send, swap_recv, meta_sem, halo_send, halo_recv, back_send, back_recv = rest[8:]
    row, col = lax.axis_index("row"), lax.axis_index("col")
    core, side = lax.rem(row, 2), lax.rem(col, 2)
    sibling = row + 1 - 2 * core
    step_row, step_col = 2 * core - 1, 2 * side - 1

    def wrapped(r, c):
        return (lax.rem(r + 64, 64), lax.rem(c + 8, 8))

    partner = (sibling, col - step_col)
    target = {
        (0, OUT_X): wrapped(sibling, col + 2 * step_col),
        (1, OUT_X): wrapped(sibling, col - 2 * step_col),
        (0, OUT_Z): wrapped(row + step_row, col),
        (1, OUT_Z): wrapped(row - 3 * step_row, col),
    }
    for region in (0, 1):
        target[region, IN_X] = target[region, IN_Z] = (sibling, col)

    loads = [
        pltpu.make_async_copy(dens_a, loaded.at[0], load_sem.at[0]),
        pltpu.make_async_copy(dens_b, loaded.at[1], load_sem.at[1]),
    ]
    for load in loads:
        load.start()
    barrier = pltpu.get_barrier_semaphore()
    greeted = (partner, (sibling, col), target[0, OUT_X], target[1, OUT_X], target[0, OUT_Z], target[1, OUT_Z])
    for device in greeted:
        pl.semaphore_signal(barrier, 1, device_id=device, device_id_type=MESH)

    names_a = names_of(codes_a, count_a, core, side)
    names_b = names_of(codes_b, count_b, core, side)
    mine = [jnp.where(side == 0, a, b) for a, b in zip(names_a, names_b)]
    theirs = [jnp.where(side == 0, b, a) for a, b in zip(names_a, names_b)]
    order_mine, _ = in_order(mine)
    order_theirs, slot_theirs = in_order(theirs)
    for index in range(SLOTS):
        meta_out[index] = order_theirs[index]

    def block(step, region, name):
        return held[step, region].at[name]

    def halo(step, region, name, which):
        landing = region if name in (OUT_Z, IN_Z) else 1 - region
        return pltpu.make_async_remote_copy(
            src_ref=block(step, region, name if which else DIAG),
            dst_ref=block(step, landing, beside(name) + which),
            send_sem=halo_send.at[step, region, name, which],
            recv_sem=halo_recv.at[step, landing, name],
            device_id=target[region, name],
            device_id_type=MESH,
        )

    def swap(index):
        return pltpu.make_async_remote_copy(
            src_ref=swap_out.at[index],
            dst_ref=swap_in.at[index],
            send_sem=swap_send.at[index],
            recv_sem=swap_recv.at[index],
            device_id=partner,
            device_id_type=MESH,
        )

    def returned(index):
        return pltpu.make_async_remote_copy(
            src_ref=fresh[1, 1].at[index],
            dst_ref=back.at[index],
            send_sem=back_send.at[index],
            recv_sem=back_recv.at[index],
            device_id=partner,
            device_id_type=MESH,
        )

    meta = pltpu.make_async_remote_copy(
        src_ref=meta_out,
        dst_ref=meta_in,
        send_sem=meta_sem.at[0],
        recv_sem=meta_sem.at[1],
        device_id=partner,
        device_id_type=MESH,
    )

    nothing = jnp.zeros((EDGE, EDGE), jnp.bfloat16)
    for region in (0, 1):
        for step in (0, 1):
            held[step, region][NONE] = nothing
            fresh[step, region][SLOTS] = nothing
    back[SLOTS] = nothing

    for load in loads:
        load.wait()
    for index in range(SLOTS):
        chosen = loaded[1 - side, slot_theirs[index]]
        swap_out[index] = jnp.where(order_theirs[index] == NONE, nothing, chosen)
    for name in range(NONE):
        at = place(mine, name)
        chosen = loaded[side, jnp.minimum(at, SLOTS - 1)]
        held[0, 0][name] = jnp.where(at == SLOTS, nothing, chosen)

    pl.semaphore_wait(barrier, len(greeted))
    meta.start()
    swap(0).start()
    halo(0, 0, OUT_X, 0).start()
    halo(0, 0, OUT_Z, 0).start()
    swap(1).start()
    halo(0, 0, OUT_X, 1).start()
    halo(0, 0, OUT_Z, 1).start()
    swap(2).start()
    for name in (IN_X, IN_Z):
        for which in (0, 1):
            halo(0, 0, name, which).start()

    meta.wait_recv()
    order_other = [meta_in[index] for index in range(SLOTS)]
    first, second, third = order_other

    swap(0).wait_recv()
    held[0, 1][OUT_X] = jnp.where(first == OUT_X, swap_in[0], nothing)
    halo(0, 1, OUT_X, 1).start()
    swap(1).wait_recv()
    held[0, 1][DIAG] = jnp.where(
        first == DIAG, swap_in[0], jnp.where(second == DIAG, swap_in[1], nothing)
    )
    for name in BESIDE:
        halo(0, 1, name, 0).start()
    swap(2).wait_recv()
    for name in (OUT_Z, IN_X, IN_Z):
        at = place(order_other, name)
        chosen = swap_in[jnp.minimum(at, SLOTS - 1)]
        held[0, 1][name] = jnp.where(at == SLOTS, nothing, chosen)
        halo(0, 1, name, 1).start()

    layout = [diagonal_first(order_mine), diagonal_first(order_other)]

    def arrived(step, region):
        for name in BESIDE:
            pair = held[step, region].at[pl.ds(beside(name), 2)]
            pltpu.make_async_copy(pair, pair, halo_recv.at[step, region, name]).wait()

    def purify(step, region, done):
        names, has = layout[region]

        def at(index):
            return held[step, region][index]

        none = [name == NONE for name in names]
        diagonal = at(DIAG)
        left = [at(name) for name in names]
        own = at(jnp.where(has, DIAG, jnp.where(none[0], NONE, beside(names[0]))))
        across = [None] + [at(jnp.where(none[i], NONE, beside(names[i]))) for i in (1, 2)]
        towards = [None] + [
            at(jnp.where(none[i] | jnp.logical_not(has), NONE, beside(names[i]) + 1)) for i in (1, 2)
        ]
        square = [
            matmul(left[0], own) + matmul(left[1], towards[1]) + matmul(left[2], towards[2]),
            matmul(diagonal, left[1]) + matmul(left[1], across[1]),
            matmul(diagonal, left[2]) + matmul(left[2], across[2]),
        ]
        low = [s.astype(jnp.bfloat16) for s in square]
        centre = jnp.where(has, low[0], nothing)
        for index in range(SLOTS):
            if index == 0:
                cube = matmul(low[0], own) + matmul(low[1], towards[1]) + matmul(low[2], towards[2])
            else:
                cube = matmul(centre, left[index]) + matmul(low[index], across[index])
            fresh[step, region][index] = (3.0 * low[index].astype(jnp.float32) - 2.0 * cube).astype(jnp.bfloat16)
            done(index)

    for region in (1, 0):
        arrived(0, region)
        purify(0, region, lambda index: None)
        for name in (DIAG, OUT_X, OUT_Z, IN_X, IN_Z):
            held[1, region][name] = fresh[0, region][place(layout[region][0], name)]
        for name in BESIDE:
            for which in (0, 1):
                halo(1, region, name, which).start()

    arrived(1, 1)
    purify(1, 1, lambda index: returned(index).start())
    arrived(1, 0)
    purify(1, 0, lambda index: None)

    def write(out, names, order, source):
        for slot in range(SLOTS):
            out[slot] = source(place(diagonal_first(order)[0], names[slot]))

    def own_result(index):
        return fresh[1, 0][index]

    def their_result(index):
        return back[index]

    @pl.when(side == 0)
    def _():
        write(out_a, mine, order_mine, own_result)

    @pl.when(side == 1)
    def _():
        write(out_b, mine, order_mine, own_result)

    for index in range(SLOTS):
        returned(index).wait_recv()

    @pl.when(side == 0)
    def _():
        write(out_b, theirs, order_theirs, their_result)

    @pl.when(side == 1)
    def _():
        write(out_a, theirs, order_theirs, their_result)

    meta.wait_send()
    for index in range(SLOTS):
        swap(index).wait_send()
        returned(index).wait_send()
    for step in (0, 1):
        for region in (0, 1):
            for name in BESIDE:
                for which in (0, 1):
                    halo(step, region, name, which).wait_send()


def per_device(dens_a, dens_b, codes_a, codes_b, counts_a, counts_b):
    stored = (SLOTS, EDGE, EDGE)
    shape = dens_a.shape
    in_vmem = pl.BlockSpec(memory_space=pltpu.VMEM)
    in_smem = pl.BlockSpec(memory_space=pltpu.SMEM)
    anywhere = pl.BlockSpec(memory_space=pl.ANY)
    new_a, new_b = pl.pallas_call(
        kernel,
        out_shape=[jax.ShapeDtypeStruct(stored, jnp.bfloat16)] * 2,
        in_specs=[anywhere, anywhere, in_smem, in_smem, in_smem, in_smem],
        out_specs=[in_vmem, in_vmem],
        scratch_shapes=[
            pltpu.VMEM((2, *stored), jnp.bfloat16),
            pltpu.VMEM(stored, jnp.bfloat16),
            pltpu.VMEM(stored, jnp.bfloat16),
            pltpu.SMEM((SLOTS,), jnp.int32),
            pltpu.SMEM((SLOTS,), jnp.int32),
            *[pltpu.VMEM((HELD, EDGE, EDGE), jnp.bfloat16)] * 4,
            *[pltpu.VMEM((SLOTS + 1, EDGE, EDGE), jnp.bfloat16)] * 5,
            pltpu.SemaphoreType.DMA((2,)),
            pltpu.SemaphoreType.DMA((SLOTS,)),
            pltpu.SemaphoreType.DMA((SLOTS,)),
            pltpu.SemaphoreType.DMA((2,)),
            pltpu.SemaphoreType.DMA((2, 2, NONE, 2)),
            pltpu.SemaphoreType.DMA((2, 2, NONE)),
            pltpu.SemaphoreType.DMA((SLOTS,)),
            pltpu.SemaphoreType.DMA((SLOTS,)),
        ],
        compiler_params=pltpu.CompilerParams(
            collective_id=0, has_side_effects=True, vmem_limit_bytes=40 * 2**20
        ),
        name="purify",
    )(
        dens_a.reshape(stored),
        dens_b.reshape(stored),
        codes_a.reshape(SLOTS),
        codes_b.reshape(SLOTS),
        counts_a.reshape(1),
        counts_b.reshape(1),
    )
    return new_a.reshape(shape), new_b.reshape(shape)


def solution(mesh):
    placed = (
        P("row", "col", None, None, None, None),
        P("row", "col", None, None, None, None),
        P("row", "col", None, None),
        P("row", "col", None, None),
        P("row", "col", None),
        P("row", "col", None),
    )
    return jax.shard_map(
        per_device,
        mesh=mesh,
        in_specs=placed,
        out_specs=(
            P("row", "col", None, None, None, None),
            P("row", "col", None, None, None, None),
        ),
        check_vma=False,
    )
```

```python
import jax
import jax.numpy as jnp
from jax import lax
from jax.experimental import pallas as pl
from jax.experimental.pallas import tpu as pltpu
from jax.sharding import PartitionSpec as P

OUT_X, DIAG, OUT_Z, IN_X, IN_Z, NONE = range(6)
BESIDE = (OUT_X, OUT_Z, IN_X, IN_Z)
MESH = pl.DeviceIdType.MESH
EDGE = 256
SLOTS = 3
HELD = 16
RELAYED = 192


def beside(name):
    return NONE + 1 + 2 * name


def names_of(codes_ref, count_ref, row_bit, col_bit):
    names = []
    for slot in range(SLOTS):
        code = codes_ref[slot]
        vertical = jnp.where(code - 1 == row_bit, OUT_Z, IN_Z)
        lateral = jnp.where(code - 3 == col_bit, OUT_X, IN_X)
        name = jnp.where(code == 0, DIAG, jnp.where(code <= 2, vertical, lateral))
        names.append(jnp.where(slot < count_ref[0], name, NONE))
    return names


def in_order(names):
    a, b, c = (names[slot] * 4 + slot for slot in range(SLOTS))
    a, b = jnp.minimum(a, b), jnp.maximum(a, b)
    b, c = jnp.minimum(b, c), jnp.maximum(b, c)
    a, b = jnp.minimum(a, b), jnp.maximum(a, b)
    return [v // 4 for v in (a, b, c)], [v % 4 for v in (a, b, c)]


def diagonal_first(order):
    first, second, third = order
    has = (first == DIAG) | (second == DIAG)
    return [jnp.where(has, DIAG, first), jnp.where(second == DIAG, first, second), third], has


def place(names, wanted):
    at = jnp.int32(SLOTS)
    for index in reversed(range(SLOTS)):
        at = jnp.where(names[index] == wanted, index, at)
    return at


def matmul(x, y):
    return jnp.dot(x, y, preferred_element_type=jnp.float32)


def kernel(
    dens_a, dens_b, *given_and_rest,
):
    given, (out_a, out_b), given_and_rest = given_and_rest[:4], given_and_rest[4:6], given_and_rest[6:]
    kept, given_and_rest = given_and_rest[:4], given_and_rest[4:]
    loaded, swap_out, swap_in, meta_out, meta_in, relay, *rest = given_and_rest
    held = {(step, region): rest[2 * step + region] for step in (0, 1) for region in (0, 1)}
    fresh = {(step, region): rest[4 + 2 * step + region] for step in (0, 1) for region in (0, 1)}
    back, load_sem, swap_send, swap_recv, meta_sem, halo_send, halo_recv, back_send, back_recv = rest[8:17]
    relay_send, relay_recv, onward_send = rest[17:]
    row, col = lax.axis_index("row"), lax.axis_index("col")
    core, side = lax.rem(row, 2), lax.rem(col, 2)
    sibling = row + 1 - 2 * core
    step_row, step_col = 2 * core - 1, 2 * side - 1

    def wrapped(r, c):
        return (lax.rem(r + 64, 64), lax.rem(c + 8, 8))

    partner = (sibling, col - step_col)
    target = {
        (0, OUT_X): wrapped(sibling, col + 2 * step_col),
        (1, OUT_X): wrapped(sibling, col - 2 * step_col),
        (0, OUT_Z): wrapped(row + step_row, col),
        (1, OUT_Z): wrapped(row - 3 * step_row, col),
    }
    for region in (0, 1):
        target[region, IN_X] = target[region, IN_Z] = (sibling, col)

    depth = lax.rem(row // 2, 8)
    first_plane, last_plane = depth == 0, depth == 7
    edge = [(first_plane & (core == region)) | (last_plane & (core != region)) for region in (0, 1)]
    across = tuple(jnp.where(edge[0], a, b) for a, b in zip(target[0, OUT_Z], target[1, OUT_Z]))
    onward = (lax.rem(row + 16, 64), col)
    behind = (lax.rem(row + 48, 64), col)
    relay_of = (row - 14 + 1 - 2 * core, col)
    relay_for = (row + 14 + 1 - 2 * core, col)

    loads = [
        pltpu.make_async_copy(source, home, load_sem.at[index])
        for index, (source, home) in enumerate(
            [*zip(given, kept), (dens_a, loaded.at[0]), (dens_b, loaded.at[1])]
        )
    ]
    for load in loads:
        load.start()
    codes_a, codes_b, count_a, count_b = kept
    barrier = pltpu.get_barrier_semaphore()

    def greet(device):
        pl.semaphore_signal(barrier, 1, device_id=device, device_id_type=MESH)

    for device in (partner, (sibling, col), target[0, OUT_X], target[1, OUT_X]):
        greet(device)
    for region in (0, 1):
        pl.when(jnp.logical_not(edge[region]))(lambda: greet(target[region, OUT_Z]))

    @pl.when(first_plane)
    def _():
        greet(behind)
        greet(relay_for)

    for load in loads[:4]:
        load.wait()
    names_a = names_of(codes_a, count_a, core, side)
    names_b = names_of(codes_b, count_b, core, side)
    mine = [jnp.where(side == 0, a, b) for a, b in zip(names_a, names_b)]
    theirs = [jnp.where(side == 0, b, a) for a, b in zip(names_a, names_b)]
    order_mine, _ = in_order(mine)
    order_theirs, slot_theirs = in_order(theirs)
    for index in range(SLOTS):
        meta_out[index] = order_theirs[index]

    def block(step, region, name):
        return held[step, region].at[name]

    def halo(step, region, name, which):
        landing = region if name in (OUT_Z, IN_Z) else 1 - region
        return pltpu.make_async_remote_copy(
            src_ref=block(step, region, name if which else DIAG),
            dst_ref=block(step, landing, beside(name) + which),
            send_sem=halo_send.at[step, region, name, which],
            recv_sem=halo_recv.at[step, landing, name],
            device_id=target[region, name],
            device_id_type=MESH,
        )

    def tail(ref):
        return ref.at[pl.ds(EDGE - RELAYED, RELAYED)]

    def head(ref):
        return ref.at[pl.ds(0, EDGE - RELAYED)]

    def halo_head(step, region):
        return pltpu.make_async_remote_copy(
            src_ref=head(block(step, region, OUT_Z)),
            dst_ref=head(block(step, region, beside(OUT_Z) + 1)),
            send_sem=halo_send.at[step, region, OUT_Z, 1],
            recv_sem=halo_recv.at[step, region, OUT_Z],
            device_id=target[region, OUT_Z],
            device_id_type=MESH,
        )

    def to_relay(step, region):
        return pltpu.make_async_remote_copy(
            src_ref=tail(block(step, region, OUT_Z)),
            dst_ref=relay.at[step],
            send_sem=relay_send.at[step],
            recv_sem=relay_recv.at[step],
            device_id=relay_of,
            device_id_type=MESH,
        )

    def from_relay(step, region):
        return pltpu.make_async_remote_copy(
            src_ref=relay.at[step],
            dst_ref=tail(block(step, region, beside(OUT_Z) + 1)),
            send_sem=onward_send.at[step],
            recv_sem=halo_recv.at[step, region, OUT_Z],
            device_id=onward,
            device_id_type=MESH,
        )

    def parts(step, region, name, which):
        whole = halo(step, region, name, which)
        if name != OUT_Z or not which:
            return [(None, whole)]
        cut = edge[region] & last_plane
        return [
            (jnp.logical_not(cut), whole),
            (cut, to_relay(step, region)),
            (cut, halo_head(step, region)),
        ]

    def send(step, region, name, which, when=None):
        for condition, copy in parts(step, region, name, which):
            both = condition if when is None else when if condition is None else condition & when
            if both is None:
                copy.start()
            else:
                pl.when(both)(copy.start)

    def pass_on(step):
        for region in (0, 1):

            @pl.when(first_plane & (core == region))
            def _():
                to_relay(step, region).wait_recv()
                from_relay(step, region).start()

    def swap(index):
        return pltpu.make_async_remote_copy(
            src_ref=swap_out.at[index],
            dst_ref=swap_in.at[index],
            send_sem=swap_send.at[index],
            recv_sem=swap_recv.at[index],
            device_id=partner,
            device_id_type=MESH,
        )

    def returned(index):
        return pltpu.make_async_remote_copy(
            src_ref=fresh[1, 1].at[index],
            dst_ref=back.at[index],
            send_sem=back_send.at[index],
            recv_sem=back_recv.at[index],
            device_id=partner,
            device_id_type=MESH,
        )

    meta = pltpu.make_async_remote_copy(
        src_ref=meta_out,
        dst_ref=meta_in,
        send_sem=meta_sem.at[0],
        recv_sem=meta_sem.at[1],
        device_id=partner,
        device_id_type=MESH,
    )

    nothing = jnp.zeros((EDGE, EDGE), jnp.bfloat16)
    for region in (0, 1):
        for step in (0, 1):
            held[step, region][NONE] = nothing
            fresh[step, region][SLOTS] = nothing
    back[SLOTS] = nothing

    for load in loads[4:]:
        load.wait()
    for index in range(SLOTS):
        chosen = loaded[1 - side, slot_theirs[index]]
        swap_out[index] = jnp.where(order_theirs[index] == NONE, nothing, chosen)
    for name in range(NONE):
        at = place(mine, name)
        chosen = loaded[side, jnp.minimum(at, SLOTS - 1)]
        held[0, 0][name] = jnp.where(at == SLOTS, nothing, chosen)

    pl.semaphore_wait(barrier, jnp.where(last_plane, 7, 6))
    pl.when(first_plane | last_plane)(lambda: greet(across))
    early = [jnp.logical_not(edge[region] & first_plane) for region in (0, 1)]
    meta.start()
    swap(0).start()
    send(0, 0, OUT_X, 0)
    swap(1).start()
    send(0, 0, OUT_X, 1)
    swap(2).start()
    for which in (0, 1):
        send(0, 0, OUT_Z, which, early[0])
    for name in (IN_X, IN_Z):
        for which in (0, 1):
            send(0, 0, name, which)

    meta.wait_recv()
    order_other = [meta_in[index] for index in range(SLOTS)]
    first, second, third = order_other

    swap(0).wait_recv()
    held[0, 1][OUT_X] = jnp.where(first == OUT_X, swap_in[0], nothing)
    send(0, 1, OUT_X, 1)
    swap(1).wait_recv()
    held[0, 1][DIAG] = jnp.where(
        first == DIAG, swap_in[0], jnp.where(second == DIAG, swap_in[1], nothing)
    )
    for name in BESIDE:
        send(0, 1, name, 0, early[1] if name == OUT_Z else None)
    swap(2).wait_recv()
    for name in (OUT_Z, IN_X, IN_Z):
        at = place(order_other, name)
        chosen = swap_in[jnp.minimum(at, SLOTS - 1)]
        held[0, 1][name] = jnp.where(at == SLOTS, nothing, chosen)
        send(0, 1, name, 1, early[1] if name == OUT_Z else None)

    @pl.when(first_plane)
    def _():
        pl.semaphore_wait(barrier, 1)

    for region in (0, 1):
        for which in (0, 1):
            pl.when(jnp.logical_not(early[region]))(halo(0, region, OUT_Z, which).start)
    pass_on(0)

    layout = [diagonal_first(order_mine), diagonal_first(order_other)]

    def arrived(step, region):
        for name in BESIDE:
            pair = held[step, region].at[pl.ds(beside(name), 2)]
            pltpu.make_async_copy(pair, pair, halo_recv.at[step, region, name]).wait()

    def purify(step, region, done):
        names, has = layout[region]

        def at(index):
            return held[step, region][index]

        none = [name == NONE for name in names]
        diagonal = at(DIAG)
        left = [at(name) for name in names]
        own = at(jnp.where(has, DIAG, jnp.where(none[0], NONE, beside(names[0]))))
        across = [None] + [at(jnp.where(none[i], NONE, beside(names[i]))) for i in (1, 2)]
        towards = [None] + [
            at(jnp.where(none[i] | jnp.logical_not(has), NONE, beside(names[i]) + 1)) for i in (1, 2)
        ]
        square = [
            matmul(left[0], own) + matmul(left[1], towards[1]) + matmul(left[2], towards[2]),
            matmul(diagonal, left[1]) + matmul(left[1], across[1]),
            matmul(diagonal, left[2]) + matmul(left[2], across[2]),
        ]
        low = [s.astype(jnp.bfloat16) for s in square]
        centre = jnp.where(has, low[0], nothing)
        for index in range(SLOTS):
            if index == 0:
                cube = matmul(low[0], own) + matmul(low[1], towards[1]) + matmul(low[2], towards[2])
            else:
                cube = matmul(centre, left[index]) + matmul(low[index], across[index])
            fresh[step, region][index] = (3.0 * low[index].astype(jnp.float32) - 2.0 * cube).astype(jnp.bfloat16)
            done(index)

    for region in (1, 0):
        arrived(0, region)
        purify(0, region, lambda index: None)
        for name in (DIAG, OUT_X, OUT_Z, IN_X, IN_Z):
            held[1, region][name] = fresh[0, region][place(layout[region][0], name)]
        for name in BESIDE:
            for which in (0, 1):
                send(1, region, name, which)

    pass_on(1)
    arrived(1, 1)
    purify(1, 1, lambda index: returned(index).start())
    arrived(1, 0)
    purify(1, 0, lambda index: None)

    def write(out, names, order, source):
        for slot in range(SLOTS):
            out[slot] = source(place(diagonal_first(order)[0], names[slot]))

    def own_result(index):
        return fresh[1, 0][index]

    def their_result(index):
        return back[index]

    @pl.when(side == 0)
    def _():
        write(out_a, mine, order_mine, own_result)

    @pl.when(side == 1)
    def _():
        write(out_b, mine, order_mine, own_result)

    for index in range(SLOTS):
        returned(index).wait_recv()

    @pl.when(side == 0)
    def _():
        write(out_b, theirs, order_theirs, their_result)

    @pl.when(side == 1)
    def _():
        write(out_a, theirs, order_theirs, their_result)

    meta.wait_send()
    for index in range(SLOTS):
        swap(index).wait_send()
        returned(index).wait_send()
    for step in (0, 1):
        for region in (0, 1):
            for name in BESIDE:
                for which in (0, 1):
                    for condition, copy in parts(step, region, name, which):
                        if condition is None:
                            copy.wait_send()
                        else:
                            pl.when(condition)(copy.wait_send)
            pl.when(first_plane & (core == region))(from_relay(step, region).wait_send)


def per_device(dens_a, dens_b, codes_a, codes_b, counts_a, counts_b):
    stored = (SLOTS, EDGE, EDGE)
    shape = dens_a.shape
    in_vmem = pl.BlockSpec(memory_space=pltpu.VMEM)
    in_hbm = pl.BlockSpec(memory_space=pltpu.HBM)
    new_a, new_b = pl.pallas_call(
        kernel,
        out_shape=[jax.ShapeDtypeStruct(stored, jnp.bfloat16)] * 2,
        in_specs=[in_hbm] * 6,
        out_specs=[in_vmem, in_vmem],
        scratch_shapes=[
            pltpu.SMEM((SLOTS,), jnp.int32),
            pltpu.SMEM((SLOTS,), jnp.int32),
            pltpu.SMEM((1,), jnp.int32),
            pltpu.SMEM((1,), jnp.int32),
            pltpu.VMEM((2, *stored), jnp.bfloat16),
            pltpu.VMEM(stored, jnp.bfloat16),
            pltpu.VMEM(stored, jnp.bfloat16),
            pltpu.SMEM((SLOTS,), jnp.int32),
            pltpu.SMEM((SLOTS,), jnp.int32),
            pltpu.VMEM((2, RELAYED, EDGE), jnp.bfloat16),
            *[pltpu.VMEM((HELD, EDGE, EDGE), jnp.bfloat16)] * 4,
            *[pltpu.VMEM((SLOTS + 1, EDGE, EDGE), jnp.bfloat16)] * 5,
            pltpu.SemaphoreType.DMA((6,)),
            pltpu.SemaphoreType.DMA((SLOTS,)),
            pltpu.SemaphoreType.DMA((SLOTS,)),
            pltpu.SemaphoreType.DMA((2,)),
            pltpu.SemaphoreType.DMA((2, 2, NONE, 2)),
            pltpu.SemaphoreType.DMA((2, 2, NONE)),
            pltpu.SemaphoreType.DMA((SLOTS,)),
            pltpu.SemaphoreType.DMA((SLOTS,)),
            pltpu.SemaphoreType.DMA((2,)),
            pltpu.SemaphoreType.DMA((2,)),
            pltpu.SemaphoreType.DMA((2,)),
        ],
        compiler_params=pltpu.CompilerParams(
            collective_id=0, has_side_effects=True, vmem_limit_bytes=62 * 2**20
        ),
        name="purify",
    )(
        dens_a.reshape(stored),
        dens_b.reshape(stored),
        codes_a.reshape(SLOTS),
        codes_b.reshape(SLOTS),
        counts_a.reshape(1),
        counts_b.reshape(1),
    )
    return new_a.reshape(shape), new_b.reshape(shape)


def solution(mesh):
    placed = (
        P("row", "col", None, None, None, None),
        P("row", "col", None, None, None, None),
        P("row", "col", None, None),
        P("row", "col", None, None),
        P("row", "col", None),
        P("row", "col", None),
    )
    return jax.shard_map(
        per_device,
        mesh=mesh,
        in_specs=placed,
        out_specs=(
            P("row", "col", None, None, None, None),
            P("row", "col", None, None, None, None),
        ),
        check_vma=False,
    )
```

```python
import functools

import jax
import jax.numpy as jnp
from jax import lax
from jax.experimental import pallas as pl
from jax.experimental.pallas import tpu as pltpu
from jax.sharding import PartitionSpec as P

OUT_X, DIAG, OUT_Z, IN_X, IN_Z, NONE = range(6)
BESIDE = (OUT_X, OUT_Z, IN_X, IN_Z)
MESH = pl.DeviceIdType.MESH
EDGE = 256
SLOTS = 3
HELD = 16
RELAYED = 192


def beside(name):
    return NONE + 1 + 2 * name


def names_of(codes_ref, count_ref, row_bit, col_bit):
    names = []
    for slot in range(SLOTS):
        code = codes_ref[slot]
        vertical = jnp.where(code - 1 == row_bit, OUT_Z, IN_Z)
        lateral = jnp.where(code - 3 == col_bit, OUT_X, IN_X)
        name = jnp.where(code == 0, DIAG, jnp.where(code <= 2, vertical, lateral))
        names.append(jnp.where(slot < count_ref[0], name, NONE))
    return names


def in_order(names):
    a, b, c = (names[slot] * 4 + slot for slot in range(SLOTS))
    a, b = jnp.minimum(a, b), jnp.maximum(a, b)
    b, c = jnp.minimum(b, c), jnp.maximum(b, c)
    a, b = jnp.minimum(a, b), jnp.maximum(a, b)
    return [v // 4 for v in (a, b, c)], [v % 4 for v in (a, b, c)]


def diagonal_first(order):
    first, second, third = order
    has = (first == DIAG) | (second == DIAG)
    return [jnp.where(has, DIAG, first), jnp.where(second == DIAG, first, second), third], has


def place(names, wanted):
    at = jnp.int32(SLOTS)
    for index in reversed(range(SLOTS)):
        at = jnp.where(names[index] == wanted, index, at)
    return at


def matmul(x, y):
    return jnp.dot(x, y, preferred_element_type=jnp.float32)


def kernel(
    dens_a, dens_b, codes_a_hbm, codes_b_hbm, count_a_hbm, count_b_hbm, out_a, out_b,
    codes_a, codes_b, count_a, count_b, loaded, swap_out, swap_in, meta_out, meta_in, up, up_late, down, down_late,
    held_00, held_01, held_10, held_11, fresh_00, fresh_01, fresh_10, fresh_11, back,
    load_sem, swap_send, swap_recv, meta_sem, halo_send, halo_recv, back_send, back_recv, via_send, via_recv,
):
    held = ((held_00, held_01), (held_10, held_11))
    fresh = ((fresh_00, fresh_01), (fresh_10, fresh_11))
    row, col = lax.axis_index("row"), lax.axis_index("col")
    core, side = lax.rem(row, 2), lax.rem(col, 2)
    own = [core == region for region in (0, 1)]
    depth = lax.rem(row // 2, 8)
    first_plane, last_plane = depth == 0, depth == 7
    sibling = row + 1 - 2 * core
    step_col = 2 * side - 1

    def wrapped(r, c):
        return (lax.rem(r + 64, 64), lax.rem(c + 8, 8))

    partner = (sibling, col - step_col)
    target = {}
    for region in (0, 1):
        target[region, OUT_X] = wrapped(sibling, col + jnp.where(own[region], 2, -2) * step_col)
        target[region, OUT_Z] = wrapped(sibling + 4 * region - 2, col)
        target[region, IN_X] = target[region, IN_Z] = (sibling, col)
    across = tuple(jnp.where(first_plane, a, b) for a, b in zip(target[0, OUT_Z], target[1, OUT_Z]))
    onward, behind = wrapped(row + 16, col), wrapped(row - 16, col)
    relay_of, relay_for = wrapped(sibling - 14, col), wrapped(sibling + 14, col)

    loads = [
        pltpu.make_async_copy(source, home, load_sem.at[index])
        for index, (source, home) in enumerate(
            (
                (codes_a_hbm, codes_a),
                (codes_b_hbm, codes_b),
                (count_a_hbm, count_a),
                (count_b_hbm, count_b),
                (dens_a, loaded.at[0]),
                (dens_b, loaded.at[1]),
            )
        )
    ]
    for load in loads:
        load.start()
    barrier = pltpu.get_barrier_semaphore()

    def greet(device):
        pl.semaphore_signal(barrier, 1, device_id=device, device_id_type=MESH)

    for device in (partner, (sibling, col), target[0, OUT_X], target[1, OUT_X]):
        greet(device)
    pl.when(jnp.logical_not(first_plane))(lambda: greet(target[0, OUT_Z]))
    pl.when(jnp.logical_not(last_plane))(lambda: greet(target[1, OUT_Z]))

    pl.when(first_plane | last_plane)(lambda: greet(onward))
    pl.when(first_plane)(lambda: greet(behind))

    nothing = jnp.zeros((EDGE, EDGE), jnp.bfloat16)
    for region in (0, 1):
        for step in (0, 1):
            held[step][region][NONE] = nothing
            fresh[step][region][SLOTS] = nothing
    back[SLOTS] = nothing

    for load in loads[:4]:
        load.wait()
    names_a = names_of(codes_a, count_a, core, side)
    names_b = names_of(codes_b, count_b, core, side)
    mine = [jnp.where(side == 0, a, b) for a, b in zip(names_a, names_b)]
    theirs = [jnp.where(side == 0, b, a) for a, b in zip(names_a, names_b)]
    order_mine, _ = in_order(mine)
    order_theirs, slot_theirs = in_order(theirs)
    for index in range(SLOTS):
        meta_out[index] = order_theirs[index]

    def remote(source, landing, sent, received, device):
        return pltpu.make_async_remote_copy(
            src_ref=source,
            dst_ref=landing,
            send_sem=sent,
            recv_sem=received,
            device_id=device,
            device_id_type=MESH,
        )

    def swap(index):
        return remote(swap_out.at[index], swap_in.at[index], swap_send.at[index], swap_recv.at[index], partner)

    def returned(region, index):
        return remote(
            fresh[1][region].at[index], back.at[index], back_send.at[index], back_recv.at[index], partner
        )

    meta = remote(meta_out, meta_in, meta_sem.at[0], meta_sem.at[1], partner)

    def landing_of(region, name):
        return 1 - region if name in (OUT_Z, IN_Z) else region

    def halo(step, region, name, which, rows=slice(0, EDGE)):
        landing = landing_of(region, name)
        cut = pl.ds(rows.start, rows.stop - rows.start)
        return remote(
            held[step][region].at[name if which else DIAG, cut],
            held[step][landing].at[beside(name) + which, cut],
            halo_send.at[step, region, name, which],
            halo_recv.at[step, landing, name],
            target[region, name],
        )

    def up_first(which):
        source = held[0][1].at[OUT_Z if which else DIAG]
        return remote(source, up.at[which], halo_send.at[0, 1, OUT_Z, which], via_recv.at[which], relay_of)

    def up_first_on(which):
        landing = held[0][0].at[beside(OUT_Z) + which]
        return remote(up.at[which], landing, via_send.at[which], halo_recv.at[0, 0, OUT_Z], onward)

    tail = pl.ds(EDGE - RELAYED, RELAYED)

    def up_second():
        return remote(held[1][1].at[OUT_Z, tail], up_late, via_send.at[5], via_recv.at[2], relay_of)

    def up_second_on():
        landing = held[1][0].at[beside(OUT_Z) + 1, tail]
        return remote(up_late, landing, via_send.at[2], halo_recv.at[1, 0, OUT_Z], onward)

    def down_first(which):
        source = held[0][0].at[OUT_Z if which else DIAG]
        return remote(source, down.at[which], halo_send.at[0, 0, OUT_Z, which], via_recv.at[3 + which], behind)

    def down_first_on(which):
        landing = held[0][1].at[beside(OUT_Z) + which]
        return remote(down.at[which], landing, via_send.at[3 + which], halo_recv.at[0, 1, OUT_Z], relay_for)

    def down_second():
        return remote(held[1][0].at[OUT_Z], down_late, halo_send.at[1, 0, OUT_Z, 1], via_recv.at[5], relay_for)

    def down_second_on():
        landing = held[1][1].at[beside(OUT_Z) + 1]
        return remote(down_late, landing, via_send.at[6], halo_recv.at[1, 1, OUT_Z], behind)

    def parts(step, region, name, which):
        whole = halo(step, region, name, which)
        if name != OUT_Z:
            return [(None, whole)]
        if step == 0:
            other = [down_first, up_first][region](which)
            cut = first_plane if region == 0 else last_plane & own[1]
            return [(cut, other), (jnp.logical_not(cut), whole)]
        if which == 0:
            return [(None, whole)]
        if region == 0:
            return [(first_plane, down_second()), (jnp.logical_not(first_plane), whole)]
        return [
            (last_plane, up_second()),
            (last_plane, halo(step, region, name, which, slice(0, EDGE - RELAYED))),
            (jnp.logical_not(last_plane), whole),
        ]

    def send(step, region, name, which):
        for condition, copy in parts(step, region, name, which):
            if condition is None:
                copy.start()
            else:
                pl.when(condition)(copy.start)

    for load in loads[4:]:
        load.wait()
    for index in range(SLOTS):
        chosen = loaded[1 - side, slot_theirs[index]]
        swap_out[index] = jnp.where(order_theirs[index] == NONE, nothing, chosen)
    for region in (0, 1):

        @pl.when(own[region])
        def _():
            for name in range(NONE):
                at = place(mine, name)
                chosen = loaded[side, jnp.minimum(at, SLOTS - 1)]
                held[0][region][name] = jnp.where(at == SLOTS, nothing, chosen)

    pl.semaphore_wait(barrier, jnp.where(first_plane, 7, jnp.where(last_plane, 8, 6)))
    pl.when(first_plane | last_plane)(lambda: greet(across))
    pl.when(first_plane)(lambda: greet(relay_for))
    pl.when(last_plane)(lambda: greet(relay_of))
    meta.start()
    for region in (0, 1):

        @pl.when(own[region])
        def _():
            swap(0).start()
            send(0, region, OUT_X, 0)
            send(0, region, OUT_Z, 0)
            swap(1).start()
            send(0, region, OUT_X, 1)
            send(0, region, OUT_Z, 1)
            swap(2).start()
            for name in (IN_X, IN_Z):
                for which in (0, 1):
                    send(0, region, name, which)

    meta.wait_recv()
    order_other = [meta_in[index] for index in range(SLOTS)]
    first, second, third = order_other
    for region in (0, 1):

        @pl.when(jnp.logical_not(own[region]))
        def _():
            swap(0).wait_recv()
            held[0][region][OUT_X] = jnp.where(first == OUT_X, swap_in[0], nothing)
            send(0, region, OUT_X, 1)
            swap(1).wait_recv()
            held[0][region][DIAG] = jnp.where(
                first == DIAG, swap_in[0], jnp.where(second == DIAG, swap_in[1], nothing)
            )
            for name in (OUT_X, OUT_Z, IN_X, IN_Z):
                send(0, region, name, 0)
            swap(2).wait_recv()
            for name in (OUT_Z, IN_Z, IN_X):
                at = place(order_other, name)
                chosen = swap_in[jnp.minimum(at, SLOTS - 1)]
                held[0][region][name] = jnp.where(at == SLOTS, nothing, chosen)
                send(0, region, name, 1)

    @pl.when(first_plane)
    def _():
        pl.semaphore_wait(barrier, 2)
        for which in (0, 1):
            down_first(which).wait_recv()
            down_first_on(which).start()

    mine_first, mine_has = diagonal_first(order_mine)
    other_first, other_has = diagonal_first(order_other)
    layout = [
        (
            [jnp.where(own[region], a, b) for a, b in zip(mine_first, other_first)],
            (own[region] & mine_has) | (jnp.logical_not(own[region]) & other_has),
        )
        for region in (0, 1)
    ]

    def arrived(step, region):
        for name in BESIDE:
            pair = held[step][region].at[pl.ds(beside(name), 2)]
            pltpu.make_async_copy(pair, pair, halo_recv.at[step, region, name]).wait()

    def purify(step, region, done):
        names, has = layout[region]

        def at(index):
            return held[step][region][index]

        none = [name == NONE for name in names]
        diagonal = at(DIAG)
        left = [at(name) for name in names]
        right = at(jnp.where(has, DIAG, jnp.where(none[0], NONE, beside(names[0]))))
        over = [None] + [at(jnp.where(none[i], NONE, beside(names[i]))) for i in (1, 2)]
        towards = [None] + [
            at(jnp.where(none[i] | jnp.logical_not(has), NONE, beside(names[i]) + 1)) for i in (1, 2)
        ]
        square = [
            matmul(left[0], right) + matmul(left[1], towards[1]) + matmul(left[2], towards[2]),
            matmul(diagonal, left[1]) + matmul(left[1], over[1]),
            matmul(diagonal, left[2]) + matmul(left[2], over[2]),
        ]
        low = [s.astype(jnp.bfloat16) for s in square]
        centre = jnp.where(has, low[0], nothing)
        for index in range(SLOTS):
            if index == 0:
                cube = matmul(low[0], right) + matmul(low[1], towards[1]) + matmul(low[2], towards[2])
            else:
                cube = matmul(centre, left[index]) + matmul(low[index], over[index])
            fresh[step][region][index] = (3.0 * low[index].astype(jnp.float32) - 2.0 * cube).astype(jnp.bfloat16)
            done(index)

    def spread(region):
        for name in range(NONE):
            held[1][region][name] = fresh[0][region][place(layout[region][0], name)]
        for which in (0, 1):
            for name in (OUT_Z, OUT_X) if region else (OUT_X, OUT_Z):
                send(1, region, name, which)
        for name in (IN_X, IN_Z):
            for which in (0, 1):
                send(1, region, name, which)

    def give_back(region, index):
        pl.when(jnp.logical_not(own[region]))(returned(region, index).start)

    @pl.when(first_plane & own[0])
    def _():
        for which in (0, 1):
            up_first(which).wait_recv()
            up_first_on(which).start()

    arrived(0, 1)
    purify(0, 1, lambda index: None)
    spread(1)

    arrived(0, 0)
    purify(0, 0, lambda index: None)
    spread(0)

    @pl.when(first_plane)
    def _():
        up_second().wait_recv()
        up_second_on().start()

    @pl.when(last_plane)
    def _():
        down_second().wait_recv()
        down_second_on().start()

    for region in (1, 0):
        arrived(1, region)
        purify(1, region, functools.partial(give_back, region))

    def write(out, names, order, source):
        for slot in range(SLOTS):
            out[slot] = source[place(diagonal_first(order)[0], names[slot])]

    outs = (out_a, out_b)
    for which_side in (0, 1):
        for region in (0, 1):

            @pl.when((side == which_side) & own[region])
            def _():
                write(outs[which_side], mine, order_mine, fresh[1][region])

    for index in range(SLOTS):
        returned(0, index).wait_recv()
    for which_side in (0, 1):

        @pl.when(side == which_side)
        def _():
            write(outs[1 - which_side], theirs, order_theirs, back)

    meta.wait_send()
    for index in range(SLOTS):
        swap(index).wait_send()
        returned(0, index).wait_send()
    for step in (0, 1):
        for region in (0, 1):
            for name in BESIDE:
                for which in (0, 1):
                    for condition, copy in parts(step, region, name, which):
                        if condition is None:
                            copy.wait_send()
                        else:
                            pl.when(condition)(copy.wait_send)

    pl.when(last_plane)(down_second_on().wait_send)

    @pl.when(first_plane)
    def _():
        up_second_on().wait_send()
        for which in (0, 1):
            down_first_on(which).wait_send()
            pl.when(own[0])(up_first_on(which).wait_send)


def per_device(dens_a, dens_b, codes_a, codes_b, counts_a, counts_b):
    stored = (SLOTS, EDGE, EDGE)
    shape = dens_a.shape
    in_vmem = pl.BlockSpec(memory_space=pltpu.VMEM)
    in_hbm = pl.BlockSpec(memory_space=pltpu.HBM)
    new_a, new_b = pl.pallas_call(
        kernel,
        out_shape=[pltpu.VMEM(stored, jnp.bfloat16)] * 2,
        in_specs=[in_hbm] * 6,
        out_specs=[in_vmem, in_vmem],
        scratch_shapes=[
            pltpu.SMEM((SLOTS,), jnp.int32),
            pltpu.SMEM((SLOTS,), jnp.int32),
            pltpu.SMEM((1,), jnp.int32),
            pltpu.SMEM((1,), jnp.int32),
            pltpu.VMEM((2, *stored), jnp.bfloat16),
            pltpu.VMEM(stored, jnp.bfloat16),
            pltpu.VMEM(stored, jnp.bfloat16),
            pltpu.SMEM((SLOTS,), jnp.int32),
            pltpu.SMEM((SLOTS,), jnp.int32),
            pltpu.VMEM((2, EDGE, EDGE), jnp.bfloat16),
            pltpu.VMEM((RELAYED, EDGE), jnp.bfloat16),
            pltpu.VMEM((2, EDGE, EDGE), jnp.bfloat16),
            pltpu.VMEM((EDGE, EDGE), jnp.bfloat16),
            *[pltpu.VMEM((HELD, EDGE, EDGE), jnp.bfloat16)] * 4,
            *[pltpu.VMEM((SLOTS + 1, EDGE, EDGE), jnp.bfloat16)] * 5,
            pltpu.SemaphoreType.DMA((6,)),
            pltpu.SemaphoreType.DMA((SLOTS,)),
            pltpu.SemaphoreType.DMA((SLOTS,)),
            pltpu.SemaphoreType.DMA((2,)),
            pltpu.SemaphoreType.DMA((2, 2, NONE, 2)),
            pltpu.SemaphoreType.DMA((2, 2, NONE)),
            pltpu.SemaphoreType.DMA((SLOTS,)),
            pltpu.SemaphoreType.DMA((SLOTS,)),
            pltpu.SemaphoreType.DMA((7,)),
            pltpu.SemaphoreType.DMA((6,)),
        ],
        compiler_params=pltpu.CompilerParams(
            collective_id=0, has_side_effects=True, vmem_limit_bytes=60 * 2**20
        ),
        name="purify",
    )(
        dens_a.reshape(stored),
        dens_b.reshape(stored),
        codes_a.reshape(SLOTS),
        codes_b.reshape(SLOTS),
        counts_a.reshape(1),
        counts_b.reshape(1),
    )
    return new_a.reshape(shape), new_b.reshape(shape)


def solution(mesh):
    placed = (
        P("row", "col", None, None, None, None),
        P("row", "col", None, None, None, None),
        P("row", "col", None, None),
        P("row", "col", None, None),
        P("row", "col", None),
        P("row", "col", None),
    )
    return jax.shard_map(
        per_device,
        mesh=mesh,
        in_specs=placed,
        out_specs=(
            P("row", "col", None, None, None, None),
            P("row", "col", None, None, None, None),
        ),
        check_vma=False,
    )
```

```python
import functools

import jax
import jax.numpy as jnp
from jax import lax
from jax.experimental import pallas as pl
from jax.experimental.pallas import tpu as pltpu
from jax.sharding import PartitionSpec as P

OUT_X, DIAG, OUT_Z, IN_X, IN_Z, NONE = range(6)
BESIDE = (OUT_X, OUT_Z, IN_X, IN_Z)
MESH = pl.DeviceIdType.MESH
EDGE = 256
SLOTS = 3
HELD = 16
RELAYED = 192


def beside(name):
    return NONE + 1 + 2 * name


def names_of(codes_ref, count_ref, row_bit, col_bit):
    names = []
    for slot in range(SLOTS):
        code = codes_ref[slot]
        vertical = jnp.where(code - 1 == row_bit, OUT_Z, IN_Z)
        lateral = jnp.where(code - 3 == col_bit, OUT_X, IN_X)
        name = jnp.where(code == 0, DIAG, jnp.where(code <= 2, vertical, lateral))
        names.append(jnp.where(slot < count_ref[0], name, NONE))
    return names


def in_order(names):
    a, b, c = (names[slot] * 4 + slot for slot in range(SLOTS))
    a, b = jnp.minimum(a, b), jnp.maximum(a, b)
    b, c = jnp.minimum(b, c), jnp.maximum(b, c)
    a, b = jnp.minimum(a, b), jnp.maximum(a, b)
    return [v // 4 for v in (a, b, c)], [v % 4 for v in (a, b, c)]


def diagonal_first(order):
    first, second, third = order
    has = (first == DIAG) | (second == DIAG)
    return [jnp.where(has, DIAG, first), jnp.where(second == DIAG, first, second), third], has


def place(names, wanted):
    at = jnp.int32(SLOTS)
    for index in reversed(range(SLOTS)):
        at = jnp.where(names[index] == wanted, index, at)
    return at


def matmul(x, y):
    return jnp.dot(x, y, preferred_element_type=jnp.float32)


def kernel(
    dens_a, dens_b, codes_a_hbm, codes_b_hbm, count_a_hbm, count_b_hbm, out_a, out_b,
    codes_a, codes_b, count_a, count_b, loaded, swap_out, swap_in, meta_out, meta_in, up, up_late, down, down_late,
    held_00, held_01, held_10, held_11, fresh_00, fresh_01, fresh_10, fresh_11, back,
    load_sem, swap_send, swap_recv, meta_sem, halo_send, halo_recv, back_send, back_recv, via_send, via_recv, turn,
):
    held = ((held_00, held_01), (held_10, held_11))
    fresh = ((fresh_00, fresh_01), (fresh_10, fresh_11))
    row, col = lax.axis_index("row"), lax.axis_index("col")
    core, side = lax.rem(row, 2), lax.rem(col, 2)
    own = [core == region for region in (0, 1)]
    depth = lax.rem(row // 2, 8)
    first_plane, last_plane = depth == 0, depth == 7
    sibling = row + 1 - 2 * core
    step_col = 2 * side - 1

    def wrapped(r, c):
        return (lax.rem(r + 64, 64), lax.rem(c + 8, 8))

    partner = (sibling, col - step_col)
    target = {}
    for region in (0, 1):
        target[region, OUT_X] = wrapped(sibling, col + jnp.where(own[region], 2, -2) * step_col)
        target[region, OUT_Z] = wrapped(sibling + 4 * region - 2, col)
        target[region, IN_X] = target[region, IN_Z] = (sibling, col)
    across = tuple(jnp.where(first_plane, a, b) for a, b in zip(target[0, OUT_Z], target[1, OUT_Z]))
    onward, behind = wrapped(row + 16, col), wrapped(row - 16, col)
    relay_of, relay_for = wrapped(sibling - 14, col), wrapped(sibling + 14, col)

    loads = [
        pltpu.make_async_copy(source, home, load_sem.at[index])
        for index, (source, home) in enumerate(
            (
                (codes_a_hbm, codes_a),
                (codes_b_hbm, codes_b),
                (count_a_hbm, count_a),
                (count_b_hbm, count_b),
                (dens_a, loaded.at[0]),
                (dens_b, loaded.at[1]),
            )
        )
    ]
    for load in loads:
        load.start()
    barrier = pltpu.get_barrier_semaphore()

    def greet(device):
        pl.semaphore_signal(barrier, 1, device_id=device, device_id_type=MESH)

    for device in (partner, (sibling, col), target[0, OUT_X], target[1, OUT_X]):
        greet(device)
    pl.when(jnp.logical_not(first_plane))(lambda: greet(target[0, OUT_Z]))
    pl.when(jnp.logical_not(last_plane))(lambda: greet(target[1, OUT_Z]))

    pl.when(first_plane | last_plane)(lambda: greet(onward))
    pl.when(first_plane)(lambda: greet(behind))

    nothing = jnp.zeros((EDGE, EDGE), jnp.bfloat16)
    for region in (0, 1):
        for step in (0, 1):
            held[step][region][NONE] = nothing
            fresh[step][region][SLOTS] = nothing
    back[SLOTS] = nothing

    for load in loads[:4]:
        load.wait()
    names_a = names_of(codes_a, count_a, core, side)
    names_b = names_of(codes_b, count_b, core, side)
    mine = [jnp.where(side == 0, a, b) for a, b in zip(names_a, names_b)]
    theirs = [jnp.where(side == 0, b, a) for a, b in zip(names_a, names_b)]
    order_mine, _ = in_order(mine)
    order_theirs, slot_theirs = in_order(theirs)
    for index in range(SLOTS):
        meta_out[index] = order_theirs[index]

    def remote(source, landing, sent, received, device):
        return pltpu.make_async_remote_copy(
            src_ref=source,
            dst_ref=landing,
            send_sem=sent,
            recv_sem=received,
            device_id=device,
            device_id_type=MESH,
        )

    def swap(index):
        return remote(swap_out.at[index], swap_in.at[index], swap_send.at[index], swap_recv.at[index], partner)

    def returned(region, index):
        return remote(
            fresh[1][region].at[index], back.at[index], back_send.at[index], back_recv.at[index], partner
        )

    meta = remote(meta_out, meta_in, meta_sem.at[0], meta_sem.at[1], partner)

    def landing_of(region, name):
        return 1 - region if name in (OUT_Z, IN_Z) else region

    def halo(step, region, name, which, rows=slice(0, EDGE)):
        landing = landing_of(region, name)
        cut = pl.ds(rows.start, rows.stop - rows.start)
        return remote(
            held[step][region].at[name if which else DIAG, cut],
            held[step][landing].at[beside(name) + which, cut],
            halo_send.at[step, region, name, which],
            halo_recv.at[step, landing, name],
            target[region, name],
        )

    def up_first(which):
        source = held[0][1].at[OUT_Z if which else DIAG]
        return remote(source, up.at[which], halo_send.at[0, 1, OUT_Z, which], via_recv.at[which], relay_of)

    def up_first_on(which):
        landing = held[0][0].at[beside(OUT_Z) + which]
        return remote(up.at[which], landing, via_send.at[which], halo_recv.at[0, 0, OUT_Z], onward)

    tail = pl.ds(EDGE - RELAYED, RELAYED)

    def up_second():
        return remote(held[1][1].at[OUT_Z, tail], up_late, via_send.at[5], via_recv.at[2], relay_of)

    def up_second_on():
        landing = held[1][0].at[beside(OUT_Z) + 1, tail]
        return remote(up_late, landing, via_send.at[2], halo_recv.at[1, 0, OUT_Z], onward)

    def down_first(which):
        source = held[0][0].at[OUT_Z if which else DIAG]
        return remote(source, down.at[which], halo_send.at[0, 0, OUT_Z, which], via_recv.at[3 + which], behind)

    def down_first_on(which):
        landing = held[0][1].at[beside(OUT_Z) + which]
        return remote(down.at[which], landing, via_send.at[3 + which], halo_recv.at[0, 1, OUT_Z], relay_for)

    def down_second():
        return remote(held[1][0].at[OUT_Z], down_late, halo_send.at[1, 0, OUT_Z, 1], via_recv.at[5], relay_for)

    def down_second_on():
        landing = held[1][1].at[beside(OUT_Z) + 1]
        return remote(down_late, landing, via_send.at[6], halo_recv.at[1, 1, OUT_Z], behind)

    def parts(step, region, name, which):
        whole = halo(step, region, name, which)
        if name != OUT_Z:
            return [(None, whole)]
        if step == 0:
            other = [down_first, up_first][region](which)
            cut = first_plane if region == 0 else last_plane if which == 0 else last_plane & own[1]
            return [(cut, other), (jnp.logical_not(cut), whole)]
        if which == 0:
            return [(None, whole)]
        if region == 0:
            return [(first_plane, down_second()), (jnp.logical_not(first_plane), whole)]
        return [
            (last_plane, up_second()),
            (last_plane, halo(step, region, name, which, slice(0, EDGE - RELAYED))),
            (jnp.logical_not(last_plane), whole),
        ]

    def send(step, region, name, which):
        for condition, copy in parts(step, region, name, which):
            if condition is None:
                copy.start()
            else:
                pl.when(condition)(copy.start)

    for load in loads[4:]:
        load.wait()
    for index in range(SLOTS):
        chosen = loaded[1 - side, slot_theirs[index]]
        swap_out[index] = jnp.where(order_theirs[index] == NONE, nothing, chosen)
    for region in (0, 1):

        @pl.when(own[region])
        def _():
            for name in range(NONE):
                at = place(mine, name)
                chosen = loaded[side, jnp.minimum(at, SLOTS - 1)]
                held[0][region][name] = jnp.where(at == SLOTS, nothing, chosen)

    pl.semaphore_wait(barrier, jnp.where(first_plane, 7, jnp.where(last_plane, 8, 6)))
    pl.when(first_plane | last_plane)(lambda: greet(across))
    pl.when(first_plane)(lambda: greet(relay_for))
    pl.when(last_plane)(lambda: greet(relay_of))
    meta.start()
    at_jump = first_plane | last_plane
    edge_row = jnp.where(last_plane, 1, 0)

    def own_halos(region, which):
        send(0, region, OUT_X, which)
        send(0, region, OUT_Z, which)

    def own_inner(region):
        for name in (IN_X, IN_Z):
            for which in (0, 1):
                send(0, region, name, which)

    for region in (0, 1):

        @pl.when(own[region] & jnp.logical_not(at_jump & (edge_row != region)))
        def _():
            swap(0).start()
            own_halos(region, 0)
            swap(1).start()
            own_halos(region, 1)
            swap(2).start()
            own_inner(region)

        @pl.when(own[region] & at_jump & (edge_row != region))
        def _():
            own_halos(region, 0)
            own_halos(region, 1)
            own_inner(region)
            pl.semaphore_wait(turn, 1)
            for index in range(SLOTS):
                swap(index).start()

    @pl.when(at_jump & (core == edge_row))
    def _():
        swap(1).wait_send()
        pl.semaphore_signal(turn, 1, device_id=(sibling, col), device_id_type=MESH)

    meta.wait_recv()
    order_other = [meta_in[index] for index in range(SLOTS)]
    first, second, third = order_other
    for region in (0, 1):

        @pl.when(jnp.logical_not(own[region]))
        def _():
            swap(0).wait_recv()
            held[0][region][OUT_X] = jnp.where(first == OUT_X, swap_in[0], nothing)
            send(0, region, OUT_X, 1)
            swap(1).wait_recv()
            held[0][region][DIAG] = jnp.where(
                first == DIAG, swap_in[0], jnp.where(second == DIAG, swap_in[1], nothing)
            )
            for name in (OUT_X, OUT_Z, IN_X, IN_Z):
                send(0, region, name, 0)
            swap(2).wait_recv()
            for name in (OUT_Z, IN_Z, IN_X):
                at = place(order_other, name)
                chosen = swap_in[jnp.minimum(at, SLOTS - 1)]
                held[0][region][name] = jnp.where(at == SLOTS, nothing, chosen)
                send(0, region, name, 1)

    @pl.when(first_plane)
    def _():
        pl.semaphore_wait(barrier, 2)
        for which in (0, 1):
            down_first(which).wait_recv()
            down_first_on(which).start()

    mine_first, mine_has = diagonal_first(order_mine)
    other_first, other_has = diagonal_first(order_other)
    layout = [
        (
            [jnp.where(own[region], a, b) for a, b in zip(mine_first, other_first)],
            (own[region] & mine_has) | (jnp.logical_not(own[region]) & other_has),
        )
        for region in (0, 1)
    ]

    def arrived(step, region):
        for name in BESIDE:
            pair = held[step][region].at[pl.ds(beside(name), 2)]
            pltpu.make_async_copy(pair, pair, halo_recv.at[step, region, name]).wait()

    def purify(step, region, done):
        names, has = layout[region]

        def at(index):
            return held[step][region][index]

        none = [name == NONE for name in names]
        diagonal = at(DIAG)
        left = [at(name) for name in names]
        right = at(jnp.where(has, DIAG, jnp.where(none[0], NONE, beside(names[0]))))
        over = [None] + [at(jnp.where(none[i], NONE, beside(names[i]))) for i in (1, 2)]
        towards = [None] + [
            at(jnp.where(none[i] | jnp.logical_not(has), NONE, beside(names[i]) + 1)) for i in (1, 2)
        ]
        square = [
            matmul(left[0], right) + matmul(left[1], towards[1]) + matmul(left[2], towards[2]),
            matmul(diagonal, left[1]) + matmul(left[1], over[1]),
            matmul(diagonal, left[2]) + matmul(left[2], over[2]),
        ]
        low = [s.astype(jnp.bfloat16) for s in square]
        centre = jnp.where(has, low[0], nothing)
        for index in range(SLOTS):
            if index == 0:
                cube = matmul(low[0], right) + matmul(low[1], towards[1]) + matmul(low[2], towards[2])
            else:
                cube = matmul(centre, left[index]) + matmul(low[index], over[index])
            fresh[step][region][index] = (3.0 * low[index].astype(jnp.float32) - 2.0 * cube).astype(jnp.bfloat16)
            done(index)

    def spread(region):
        for name in range(NONE):
            held[1][region][name] = fresh[0][region][place(layout[region][0], name)]
        for which in (0, 1):
            for name in (OUT_Z, OUT_X) if region else (OUT_X, OUT_Z):
                send(1, region, name, which)
        for name in (IN_X, IN_Z):
            for which in (0, 1):
                send(1, region, name, which)

    def give_back(region, index):
        pl.when(jnp.logical_not(own[region]))(returned(region, index).start)

    @pl.when(first_plane)
    def _():
        up_first(0).wait_recv()
        up_first_on(0).start()

    @pl.when(first_plane & own[0])
    def _():
        up_first(1).wait_recv()
        up_first_on(1).start()

    arrived(0, 1)
    purify(0, 1, lambda index: None)
    spread(1)

    arrived(0, 0)
    purify(0, 0, lambda index: None)
    spread(0)

    @pl.when(first_plane)
    def _():
        up_second().wait_recv()
        up_second_on().start()

    @pl.when(last_plane)
    def _():
        down_second().wait_recv()
        down_second_on().start()

    for region in (1, 0):
        arrived(1, region)
        purify(1, region, functools.partial(give_back, region))

    def write(out, names, order, source):
        for slot in range(SLOTS):
            out[slot] = source[place(diagonal_first(order)[0], names[slot])]

    outs = (out_a, out_b)
    for which_side in (0, 1):
        for region in (0, 1):

            @pl.when((side == which_side) & own[region])
            def _():
                write(outs[which_side], mine, order_mine, fresh[1][region])

    for index in range(SLOTS):
        returned(0, index).wait_recv()
    for which_side in (0, 1):

        @pl.when(side == which_side)
        def _():
            write(outs[1 - which_side], theirs, order_theirs, back)

    meta.wait_send()
    for index in range(SLOTS):
        if index == 1:
            pl.when(jnp.logical_not(at_jump & (core == edge_row)))(swap(index).wait_send)
        else:
            swap(index).wait_send()
        returned(0, index).wait_send()
    for step in (0, 1):
        for region in (0, 1):
            for name in BESIDE:
                for which in (0, 1):
                    for condition, copy in parts(step, region, name, which):
                        if condition is None:
                            copy.wait_send()
                        else:
                            pl.when(condition)(copy.wait_send)

    pl.when(last_plane)(down_second_on().wait_send)

    @pl.when(first_plane)
    def _():
        up_second_on().wait_send()
        up_first_on(0).wait_send()
        pl.when(own[0])(up_first_on(1).wait_send)
        for which in (0, 1):
            down_first_on(which).wait_send()


def per_device(dens_a, dens_b, codes_a, codes_b, counts_a, counts_b):
    stored = (SLOTS, EDGE, EDGE)
    shape = dens_a.shape
    in_vmem = pl.BlockSpec(memory_space=pltpu.VMEM)
    in_hbm = pl.BlockSpec(memory_space=pltpu.HBM)
    new_a, new_b = pl.pallas_call(
        kernel,
        out_shape=[pltpu.VMEM(stored, jnp.bfloat16)] * 2,
        in_specs=[in_hbm] * 6,
        out_specs=[in_vmem, in_vmem],
        scratch_shapes=[
            pltpu.SMEM((SLOTS,), jnp.int32),
            pltpu.SMEM((SLOTS,), jnp.int32),
            pltpu.SMEM((1,), jnp.int32),
            pltpu.SMEM((1,), jnp.int32),
            pltpu.VMEM((2, *stored), jnp.bfloat16),
            pltpu.VMEM(stored, jnp.bfloat16),
            pltpu.VMEM(stored, jnp.bfloat16),
            pltpu.SMEM((SLOTS,), jnp.int32),
            pltpu.SMEM((SLOTS,), jnp.int32),
            pltpu.VMEM((2, EDGE, EDGE), jnp.bfloat16),
            pltpu.VMEM((RELAYED, EDGE), jnp.bfloat16),
            pltpu.VMEM((2, EDGE, EDGE), jnp.bfloat16),
            pltpu.VMEM((EDGE, EDGE), jnp.bfloat16),
            *[pltpu.VMEM((HELD, EDGE, EDGE), jnp.bfloat16)] * 4,
            *[pltpu.VMEM((SLOTS + 1, EDGE, EDGE), jnp.bfloat16)] * 5,
            pltpu.SemaphoreType.DMA((6,)),
            pltpu.SemaphoreType.DMA((SLOTS,)),
            pltpu.SemaphoreType.DMA((SLOTS,)),
            pltpu.SemaphoreType.DMA((2,)),
            pltpu.SemaphoreType.DMA((2, 2, NONE, 2)),
            pltpu.SemaphoreType.DMA((2, 2, NONE)),
            pltpu.SemaphoreType.DMA((SLOTS,)),
            pltpu.SemaphoreType.DMA((SLOTS,)),
            pltpu.SemaphoreType.DMA((7,)),
            pltpu.SemaphoreType.DMA((6,)),
            pltpu.SemaphoreType.REGULAR,
        ],
        compiler_params=pltpu.CompilerParams(
            collective_id=0, has_side_effects=True, vmem_limit_bytes=60 * 2**20
        ),
        name="purify",
    )(
        dens_a.reshape(stored),
        dens_b.reshape(stored),
        codes_a.reshape(SLOTS),
        codes_b.reshape(SLOTS),
        counts_a.reshape(1),
        counts_b.reshape(1),
    )
    return new_a.reshape(shape), new_b.reshape(shape)


def solution(mesh):
    placed = (
        P("row", "col", None, None, None, None),
        P("row", "col", None, None, None, None),
        P("row", "col", None, None),
        P("row", "col", None, None),
        P("row", "col", None),
        P("row", "col", None),
    )
    return jax.shard_map(
        per_device,
        mesh=mesh,
        in_specs=placed,
        out_specs=(
            P("row", "col", None, None, None, None),
            P("row", "col", None, None, None, None),
        ),
        check_vma=False,
    )
```

```python
import functools

import jax
import jax.numpy as jnp
from jax import lax
from jax.experimental import pallas as pl
from jax.experimental.pallas import tpu as pltpu
from jax.sharding import PartitionSpec as P

OUT_X, DIAG, OUT_Z, IN_X, IN_Z, NONE = range(6)
BESIDE = (OUT_X, OUT_Z, IN_X, IN_Z)
MESH = pl.DeviceIdType.MESH
EDGE = 256
SLOTS = 3
HELD = 16
RELAYED = 192


def beside(name):
    return NONE + 1 + 2 * name


def names_of(codes_ref, count_ref, row_bit, col_bit):
    names = []
    for slot in range(SLOTS):
        code = codes_ref[slot]
        vertical = jnp.where(code - 1 == row_bit, OUT_Z, IN_Z)
        lateral = jnp.where(code - 3 == col_bit, OUT_X, IN_X)
        name = jnp.where(code == 0, DIAG, jnp.where(code <= 2, vertical, lateral))
        names.append(jnp.where(slot < count_ref[0], name, NONE))
    return names


def in_order(names):
    a, b, c = (names[slot] * 4 + slot for slot in range(SLOTS))
    a, b = jnp.minimum(a, b), jnp.maximum(a, b)
    b, c = jnp.minimum(b, c), jnp.maximum(b, c)
    a, b = jnp.minimum(a, b), jnp.maximum(a, b)
    return [v // 4 for v in (a, b, c)], [v % 4 for v in (a, b, c)]


def diagonal_first(order):
    first, second, third = order
    has = (first == DIAG) | (second == DIAG)
    return [jnp.where(has, DIAG, first), jnp.where(second == DIAG, first, second), third], has


def place(names, wanted):
    at = jnp.int32(SLOTS)
    for index in reversed(range(SLOTS)):
        at = jnp.where(names[index] == wanted, index, at)
    return at


def matmul(x, y):
    return jnp.dot(x, y, preferred_element_type=jnp.float32)


def kernel(
    dens_a, dens_b, codes_a_hbm, codes_b_hbm, count_a_hbm, count_b_hbm, out_a, out_b,
    codes_a, codes_b, count_a, count_b, loaded, swap_out, swap_in, meta_out, meta_in, up, up_late, down, down_late, down_mid,
    held_00, held_01, held_10, held_11, fresh_00, fresh_01, fresh_10, fresh_11, back,
    load_sem, swap_send, swap_recv, meta_sem, halo_send, halo_recv, back_send, back_recv, via_send, via_recv, turn,
):
    held = ((held_00, held_01), (held_10, held_11))
    fresh = ((fresh_00, fresh_01), (fresh_10, fresh_11))
    row, col = lax.axis_index("row"), lax.axis_index("col")
    core, side = lax.rem(row, 2), lax.rem(col, 2)
    own = [core == region for region in (0, 1)]
    depth = lax.rem(row // 2, 8)
    first_plane, last_plane = depth == 0, depth == 7
    sibling = row + 1 - 2 * core
    step_col = 2 * side - 1

    def wrapped(r, c):
        return (lax.rem(r + 64, 64), lax.rem(c + 8, 8))

    partner = (sibling, col - step_col)
    target = {}
    for region in (0, 1):
        target[region, OUT_X] = wrapped(sibling, col + jnp.where(own[region], 2, -2) * step_col)
        target[region, OUT_Z] = wrapped(sibling + 4 * region - 2, col)
        target[region, IN_X] = target[region, IN_Z] = (sibling, col)
    across = tuple(jnp.where(first_plane, a, b) for a, b in zip(target[0, OUT_Z], target[1, OUT_Z]))
    onward, behind = wrapped(row + 16, col), wrapped(row - 16, col)
    relay_of, relay_for = wrapped(sibling - 14, col), wrapped(sibling + 14, col)

    loads = [
        pltpu.make_async_copy(source, home, load_sem.at[index])
        for index, (source, home) in enumerate(
            (
                (codes_a_hbm, codes_a),
                (codes_b_hbm, codes_b),
                (count_a_hbm, count_a),
                (count_b_hbm, count_b),
                (dens_a, loaded.at[0]),
                (dens_b, loaded.at[1]),
            )
        )
    ]
    for load in loads:
        load.start()
    barrier = pltpu.get_barrier_semaphore()

    def greet(device):
        pl.semaphore_signal(barrier, 1, device_id=device, device_id_type=MESH)

    for device in (partner, (sibling, col), target[0, OUT_X], target[1, OUT_X]):
        greet(device)
    pl.when(jnp.logical_not(first_plane))(lambda: greet(target[0, OUT_Z]))
    pl.when(jnp.logical_not(last_plane))(lambda: greet(target[1, OUT_Z]))

    pl.when(first_plane | last_plane)(lambda: greet(onward))
    pl.when(first_plane)(lambda: greet(behind))

    nothing = jnp.zeros((EDGE, EDGE), jnp.bfloat16)
    for region in (0, 1):
        for step in (0, 1):
            held[step][region][NONE] = nothing
            fresh[step][region][SLOTS] = nothing
    back[SLOTS] = nothing

    for load in loads[:4]:
        load.wait()
    names_a = names_of(codes_a, count_a, core, side)
    names_b = names_of(codes_b, count_b, core, side)
    mine = [jnp.where(side == 0, a, b) for a, b in zip(names_a, names_b)]
    theirs = [jnp.where(side == 0, b, a) for a, b in zip(names_a, names_b)]
    order_mine, _ = in_order(mine)
    order_theirs, slot_theirs = in_order(theirs)
    for index in range(SLOTS):
        meta_out[index] = order_theirs[index]

    def remote(source, landing, sent, received, device):
        return pltpu.make_async_remote_copy(
            src_ref=source,
            dst_ref=landing,
            send_sem=sent,
            recv_sem=received,
            device_id=device,
            device_id_type=MESH,
        )

    def swap(index):
        return remote(swap_out.at[index], swap_in.at[index], swap_send.at[index], swap_recv.at[index], partner)

    def returned(region, index):
        return remote(
            fresh[1][region].at[index], back.at[index], back_send.at[index], back_recv.at[index], partner
        )

    meta = remote(meta_out, meta_in, meta_sem.at[0], meta_sem.at[1], partner)

    def landing_of(region, name):
        return 1 - region if name in (OUT_Z, IN_Z) else region

    def halo(step, region, name, which, rows=slice(0, EDGE)):
        landing = landing_of(region, name)
        cut = pl.ds(rows.start, rows.stop - rows.start)
        return remote(
            held[step][region].at[name if which else DIAG, cut],
            held[step][landing].at[beside(name) + which, cut],
            halo_send.at[step, region, name, which],
            halo_recv.at[step, landing, name],
            target[region, name],
        )

    def up_first(which):
        source = held[0][1].at[OUT_Z if which else DIAG]
        return remote(source, up.at[which], halo_send.at[0, 1, OUT_Z, which], via_recv.at[which], relay_of)

    def up_first_on(which):
        landing = held[0][0].at[beside(OUT_Z) + which]
        return remote(up.at[which], landing, via_send.at[which], halo_recv.at[0, 0, OUT_Z], onward)

    tail = pl.ds(EDGE - RELAYED, RELAYED)

    def up_second():
        return remote(held[1][1].at[OUT_Z, tail], up_late, via_send.at[5], via_recv.at[2], relay_of)

    def up_second_on():
        landing = held[1][0].at[beside(OUT_Z) + 1, tail]
        return remote(up_late, landing, via_send.at[2], halo_recv.at[1, 0, OUT_Z], onward)

    def down_first(which):
        source = held[0][0].at[OUT_Z if which else DIAG]
        return remote(source, down.at[which], halo_send.at[0, 0, OUT_Z, which], via_recv.at[3 + which], behind)

    def down_first_on(which):
        landing = held[0][1].at[beside(OUT_Z) + which]
        return remote(down.at[which], landing, via_send.at[3 + which], halo_recv.at[0, 1, OUT_Z], relay_for)

    def down_second():
        return remote(held[1][0].at[OUT_Z], down_late, halo_send.at[1, 0, OUT_Z, 1], via_recv.at[5], relay_for)

    def down_second_on():
        landing = held[1][1].at[beside(OUT_Z) + 1]
        return remote(down_late, landing, via_send.at[6], halo_recv.at[1, 1, OUT_Z], behind)

    def down_own():
        source = held[0][0].at[OUT_Z]
        return remote(source, down_mid, halo_send.at[0, 0, OUT_Z, 1], via_recv.at[6], relay_for)

    def down_own_on():
        landing = held[0][1].at[beside(OUT_Z) + 1]
        return remote(down_mid, landing, via_send.at[7], halo_recv.at[0, 1, OUT_Z], behind)

    def parts(step, region, name, which):
        whole = halo(step, region, name, which)
        if name != OUT_Z:
            return [(None, whole)]
        if step == 0:
            other = [down_first, up_first][region](which)
            if region == 0 and which == 1:
                return [(first_plane & own[1], other), (jnp.logical_not(first_plane), whole)]
            cut = first_plane if region == 0 else last_plane if which == 0 else last_plane & own[1]
            return [(cut, other), (jnp.logical_not(cut), whole)]
        if which == 0:
            return [(None, whole)]
        if region == 0:
            return [(first_plane, down_second()), (jnp.logical_not(first_plane), whole)]
        return [
            (last_plane, up_second()),
            (last_plane, halo(step, region, name, which, slice(0, EDGE - RELAYED))),
            (jnp.logical_not(last_plane), whole),
        ]

    def send(step, region, name, which):
        for condition, copy in parts(step, region, name, which):
            if condition is None:
                copy.start()
            else:
                pl.when(condition)(copy.start)

    for load in loads[4:]:
        load.wait()
    for index in range(SLOTS):
        chosen = loaded[1 - side, slot_theirs[index]]
        swap_out[index] = jnp.where(order_theirs[index] == NONE, nothing, chosen)
    for region in (0, 1):

        @pl.when(own[region])
        def _():
            for name in range(NONE):
                at = place(mine, name)
                chosen = loaded[side, jnp.minimum(at, SLOTS - 1)]
                held[0][region][name] = jnp.where(at == SLOTS, nothing, chosen)

    pl.semaphore_wait(barrier, jnp.where(first_plane, 7, jnp.where(last_plane, 8, 6)))
    pl.when(first_plane | last_plane)(lambda: greet(across))
    pl.when(first_plane)(lambda: greet(relay_for))
    pl.when(last_plane)(lambda: greet(relay_of))
    meta.start()
    at_jump = first_plane | last_plane
    edge_row = jnp.where(last_plane, 1, 0)

    def own_halos(region, which):
        send(0, region, OUT_X, which)
        send(0, region, OUT_Z, which)

    def own_inner(region):
        for name in (IN_X, IN_Z):
            for which in (0, 1):
                send(0, region, name, which)

    for region in (0, 1):

        @pl.when(own[region] & jnp.logical_not(at_jump & (edge_row != region)))
        def _():
            swap(0).start()
            own_halos(region, 0)
            swap(1).start()
            own_halos(region, 1)
            swap(2).start()
            own_inner(region)

        @pl.when(own[region] & at_jump & (edge_row != region))
        def _():
            own_halos(region, 0)
            own_halos(region, 1)
            own_inner(region)
            pl.semaphore_wait(turn, 1)
            for index in range(SLOTS):
                swap(index).start()

    @pl.when(at_jump & (core == edge_row))
    def _():
        swap(1).wait_send()
        pl.semaphore_signal(turn, 1, device_id=(sibling, col), device_id_type=MESH)

    meta.wait_recv()
    order_other = [meta_in[index] for index in range(SLOTS)]
    first, second, third = order_other
    for region in (0, 1):

        @pl.when(jnp.logical_not(own[region]))
        def _():
            swap(0).wait_recv()
            held[0][region][OUT_X] = jnp.where(first == OUT_X, swap_in[0], nothing)
            send(0, region, OUT_X, 1)
            swap(1).wait_recv()
            held[0][region][DIAG] = jnp.where(
                first == DIAG, swap_in[0], jnp.where(second == DIAG, swap_in[1], nothing)
            )
            for name in (OUT_X, OUT_Z, IN_X, IN_Z):
                send(0, region, name, 0)
            swap(2).wait_recv()
            for name in (OUT_Z, IN_Z, IN_X):
                at = place(order_other, name)
                chosen = swap_in[jnp.minimum(at, SLOTS - 1)]
                held[0][region][name] = jnp.where(at == SLOTS, nothing, chosen)
                send(0, region, name, 1)

    @pl.when(first_plane)
    def _():
        pl.semaphore_wait(barrier, 2)
        pl.when(own[0])(down_own().start)
        down_first(0).wait_recv()
        down_first_on(0).start()

    @pl.when(first_plane & own[1])
    def _():
        down_first(1).wait_recv()
        down_first_on(1).start()

    @pl.when(last_plane & own[1])
    def _():
        down_own().wait_recv()
        down_own_on().start()

    mine_first, mine_has = diagonal_first(order_mine)
    other_first, other_has = diagonal_first(order_other)
    layout = [
        (
            [jnp.where(own[region], a, b) for a, b in zip(mine_first, other_first)],
            (own[region] & mine_has) | (jnp.logical_not(own[region]) & other_has),
        )
        for region in (0, 1)
    ]

    def arrived(step, region):
        for name in BESIDE:
            pair = held[step][region].at[pl.ds(beside(name), 2)]
            pltpu.make_async_copy(pair, pair, halo_recv.at[step, region, name]).wait()

    def purify(step, region, done):
        names, has = layout[region]

        def at(index):
            return held[step][region][index]

        none = [name == NONE for name in names]
        diagonal = at(DIAG)
        left = [at(name) for name in names]
        right = at(jnp.where(has, DIAG, jnp.where(none[0], NONE, beside(names[0]))))
        over = [None] + [at(jnp.where(none[i], NONE, beside(names[i]))) for i in (1, 2)]
        towards = [None] + [
            at(jnp.where(none[i] | jnp.logical_not(has), NONE, beside(names[i]) + 1)) for i in (1, 2)
        ]
        square = [
            matmul(left[0], right) + matmul(left[1], towards[1]) + matmul(left[2], towards[2]),
            matmul(diagonal, left[1]) + matmul(left[1], over[1]),
            matmul(diagonal, left[2]) + matmul(left[2], over[2]),
        ]
        low = [s.astype(jnp.bfloat16) for s in square]
        centre = jnp.where(has, low[0], nothing)
        for index in range(SLOTS):
            if index == 0:
                cube = matmul(low[0], right) + matmul(low[1], towards[1]) + matmul(low[2], towards[2])
            else:
                cube = matmul(centre, left[index]) + matmul(low[index], over[index])
            fresh[step][region][index] = (3.0 * low[index].astype(jnp.float32) - 2.0 * cube).astype(jnp.bfloat16)
            done(index)

    def spread(region):
        for name in range(NONE):
            held[1][region][name] = fresh[0][region][place(layout[region][0], name)]
        for which in (0, 1):
            for name in (OUT_Z, OUT_X) if region else (OUT_X, OUT_Z):
                send(1, region, name, which)
        for name in (IN_X, IN_Z):
            for which in (0, 1):
                send(1, region, name, which)

    def give_back(region, index):
        pl.when(jnp.logical_not(own[region]))(returned(region, index).start)

    @pl.when(first_plane)
    def _():
        up_first(0).wait_recv()
        up_first_on(0).start()

    @pl.when(first_plane & own[0])
    def _():
        up_first(1).wait_recv()
        up_first_on(1).start()

    arrived(0, 1)
    purify(0, 1, lambda index: None)
    spread(1)

    arrived(0, 0)
    purify(0, 0, lambda index: None)
    spread(0)

    @pl.when(first_plane)
    def _():
        up_second().wait_recv()
        up_second_on().start()

    @pl.when(last_plane)
    def _():
        down_second().wait_recv()
        down_second_on().start()

    def finish(region):
        arrived(1, region)
        purify(1, region, functools.partial(give_back, region))

    pl.when(last_plane)(lambda: finish(0))
    finish(1)
    pl.when(jnp.logical_not(last_plane))(lambda: finish(0))

    def write(out, names, order, source):
        for slot in range(SLOTS):
            out[slot] = source[place(diagonal_first(order)[0], names[slot])]

    outs = (out_a, out_b)
    for which_side in (0, 1):
        for region in (0, 1):

            @pl.when((side == which_side) & own[region])
            def _():
                write(outs[which_side], mine, order_mine, fresh[1][region])

    for index in range(SLOTS):
        returned(0, index).wait_recv()
    for which_side in (0, 1):

        @pl.when(side == which_side)
        def _():
            write(outs[1 - which_side], theirs, order_theirs, back)

    meta.wait_send()
    for index in range(SLOTS):
        if index == 1:
            pl.when(jnp.logical_not(at_jump & (core == edge_row)))(swap(index).wait_send)
        else:
            swap(index).wait_send()
        returned(0, index).wait_send()
    for step in (0, 1):
        for region in (0, 1):
            for name in BESIDE:
                for which in (0, 1):
                    for condition, copy in parts(step, region, name, which):
                        if condition is None:
                            copy.wait_send()
                        else:
                            pl.when(condition)(copy.wait_send)

    pl.when(last_plane)(down_second_on().wait_send)

    @pl.when(first_plane)
    def _():
        up_second_on().wait_send()
        up_first_on(0).wait_send()
        pl.when(own[0])(up_first_on(1).wait_send)
        down_first_on(0).wait_send()
        pl.when(own[0])(down_own().wait_send)
        pl.when(own[1])(down_first_on(1).wait_send)

    pl.when(last_plane & own[1])(down_own_on().wait_send)


def per_device(dens_a, dens_b, codes_a, codes_b, counts_a, counts_b):
    stored = (SLOTS, EDGE, EDGE)
    shape = dens_a.shape
    in_vmem = pl.BlockSpec(memory_space=pltpu.VMEM)
    in_hbm = pl.BlockSpec(memory_space=pltpu.HBM)
    new_a, new_b = pl.pallas_call(
        kernel,
        out_shape=[pltpu.VMEM(stored, jnp.bfloat16)] * 2,
        in_specs=[in_hbm] * 6,
        out_specs=[in_vmem, in_vmem],
        scratch_shapes=[
            pltpu.SMEM((SLOTS,), jnp.int32),
            pltpu.SMEM((SLOTS,), jnp.int32),
            pltpu.SMEM((1,), jnp.int32),
            pltpu.SMEM((1,), jnp.int32),
            pltpu.VMEM((2, *stored), jnp.bfloat16),
            pltpu.VMEM(stored, jnp.bfloat16),
            pltpu.VMEM(stored, jnp.bfloat16),
            pltpu.SMEM((SLOTS,), jnp.int32),
            pltpu.SMEM((SLOTS,), jnp.int32),
            pltpu.VMEM((2, EDGE, EDGE), jnp.bfloat16),
            pltpu.VMEM((RELAYED, EDGE), jnp.bfloat16),
            pltpu.VMEM((2, EDGE, EDGE), jnp.bfloat16),
            pltpu.VMEM((EDGE, EDGE), jnp.bfloat16),
            pltpu.VMEM((EDGE, EDGE), jnp.bfloat16),
            *[pltpu.VMEM((HELD, EDGE, EDGE), jnp.bfloat16)] * 4,
            *[pltpu.VMEM((SLOTS + 1, EDGE, EDGE), jnp.bfloat16)] * 5,
            pltpu.SemaphoreType.DMA((6,)),
            pltpu.SemaphoreType.DMA((SLOTS,)),
            pltpu.SemaphoreType.DMA((SLOTS,)),
            pltpu.SemaphoreType.DMA((2,)),
            pltpu.SemaphoreType.DMA((2, 2, NONE, 2)),
            pltpu.SemaphoreType.DMA((2, 2, NONE)),
            pltpu.SemaphoreType.DMA((SLOTS,)),
            pltpu.SemaphoreType.DMA((SLOTS,)),
            pltpu.SemaphoreType.DMA((8,)),
            pltpu.SemaphoreType.DMA((7,)),
            pltpu.SemaphoreType.REGULAR,
        ],
        compiler_params=pltpu.CompilerParams(
            collective_id=0, has_side_effects=True, vmem_limit_bytes=60 * 2**20
        ),
        name="purify",
    )(
        dens_a.reshape(stored),
        dens_b.reshape(stored),
        codes_a.reshape(SLOTS),
        codes_b.reshape(SLOTS),
        counts_a.reshape(1),
        counts_b.reshape(1),
    )
    return new_a.reshape(shape), new_b.reshape(shape)


def solution(mesh):
    placed = (
        P("row", "col", None, None, None, None),
        P("row", "col", None, None, None, None),
        P("row", "col", None, None),
        P("row", "col", None, None),
        P("row", "col", None),
        P("row", "col", None),
    )
    return jax.shard_map(
        per_device,
        mesh=mesh,
        in_specs=placed,
        out_specs=(
            P("row", "col", None, None, None, None),
            P("row", "col", None, None, None, None),
        ),
        check_vma=False,
    )
```

```python
import functools

import jax
import jax.numpy as jnp
from jax import lax
from jax.experimental import pallas as pl
from jax.experimental.pallas import tpu as pltpu
from jax.sharding import PartitionSpec as P

OUT_X, DIAG, OUT_Z, IN_X, IN_Z, NONE = range(6)
BESIDE = (OUT_X, OUT_Z, IN_X, IN_Z)
MESH = pl.DeviceIdType.MESH
EDGE = 256
SLOTS = 3
HELD = 16
RELAYED = 128


def beside(name):
    return NONE + 1 + 2 * name


def names_of(codes_ref, count_ref, row_bit, col_bit):
    names = []
    for slot in range(SLOTS):
        code = codes_ref[slot]
        vertical = jnp.where(code - 1 == row_bit, OUT_Z, IN_Z)
        lateral = jnp.where(code - 3 == col_bit, OUT_X, IN_X)
        name = jnp.where(code == 0, DIAG, jnp.where(code <= 2, vertical, lateral))
        names.append(jnp.where(slot < count_ref[0], name, NONE))
    return names


def in_order(names):
    a, b, c = (names[slot] * 4 + slot for slot in range(SLOTS))
    a, b = jnp.minimum(a, b), jnp.maximum(a, b)
    b, c = jnp.minimum(b, c), jnp.maximum(b, c)
    a, b = jnp.minimum(a, b), jnp.maximum(a, b)
    return [v // 4 for v in (a, b, c)], [v % 4 for v in (a, b, c)]


def diagonal_first(order):
    first, second, third = order
    has = (first == DIAG) | (second == DIAG)
    return [jnp.where(has, DIAG, first), jnp.where(second == DIAG, first, second), third], has


def place(names, wanted):
    at = jnp.int32(SLOTS)
    for index in reversed(range(SLOTS)):
        at = jnp.where(names[index] == wanted, index, at)
    return at


def matmul(x, y):
    return jnp.dot(x, y, preferred_element_type=jnp.float32)


def kernel(
    dens_a, dens_b, codes_a_hbm, codes_b_hbm, count_a_hbm, count_b_hbm, out_a, out_b,
    codes_a, codes_b, count_a, count_b, loaded, swap_out, swap_in, meta_out, meta_in, up, up_late, down, down_late, down_mid,
    held_00, held_01, held_10, held_11, fresh_00, fresh_01, fresh_10, fresh_11, back,
    load_sem, swap_send, swap_recv, meta_sem, halo_send, halo_recv, back_send, back_recv, via_send, via_recv, turn,
):
    held = ((held_00, held_01), (held_10, held_11))
    fresh = ((fresh_00, fresh_01), (fresh_10, fresh_11))
    row, col = lax.axis_index("row"), lax.axis_index("col")
    core, side = lax.rem(row, 2), lax.rem(col, 2)
    own = [core == region for region in (0, 1)]
    depth = lax.rem(row // 2, 8)
    first_plane, last_plane = depth == 0, depth == 7
    sibling = row + 1 - 2 * core
    step_col = 2 * side - 1

    def wrapped(r, c):
        return (lax.rem(r + 64, 64), lax.rem(c + 8, 8))

    partner = (sibling, col - step_col)
    target = {}
    for region in (0, 1):
        target[region, OUT_X] = wrapped(sibling, col + jnp.where(own[region], 2, -2) * step_col)
        target[region, OUT_Z] = wrapped(sibling + 4 * region - 2, col)
        target[region, IN_X] = target[region, IN_Z] = (sibling, col)
    across = tuple(jnp.where(first_plane, a, b) for a, b in zip(target[0, OUT_Z], target[1, OUT_Z]))
    onward, behind = wrapped(row + 16, col), wrapped(row - 16, col)
    relay_of, relay_for = wrapped(sibling - 14, col), wrapped(sibling + 14, col)

    loads = [
        pltpu.make_async_copy(source, home, load_sem.at[index])
        for index, (source, home) in enumerate(
            (
                (codes_a_hbm, codes_a),
                (codes_b_hbm, codes_b),
                (count_a_hbm, count_a),
                (count_b_hbm, count_b),
                (dens_a, loaded.at[0]),
                (dens_b, loaded.at[1]),
            )
        )
    ]
    for load in loads:
        load.start()
    barrier = pltpu.get_barrier_semaphore()

    def greet(device):
        pl.semaphore_signal(barrier, 1, device_id=device, device_id_type=MESH)

    for device in (partner, (sibling, col), target[0, OUT_X], target[1, OUT_X]):
        greet(device)
    pl.when(jnp.logical_not(first_plane))(lambda: greet(target[0, OUT_Z]))
    pl.when(jnp.logical_not(last_plane))(lambda: greet(target[1, OUT_Z]))

    pl.when(first_plane | last_plane)(lambda: greet(onward))
    pl.when(first_plane)(lambda: greet(behind))

    nothing = jnp.zeros((EDGE, EDGE), jnp.bfloat16)
    for region in (0, 1):
        for step in (0, 1):
            held[step][region][NONE] = nothing
            fresh[step][region][SLOTS] = nothing
    back[SLOTS] = nothing

    for load in loads[:4]:
        load.wait()
    names_a = names_of(codes_a, count_a, core, side)
    names_b = names_of(codes_b, count_b, core, side)
    mine = [jnp.where(side == 0, a, b) for a, b in zip(names_a, names_b)]
    theirs = [jnp.where(side == 0, b, a) for a, b in zip(names_a, names_b)]
    order_mine, _ = in_order(mine)
    order_theirs, slot_theirs = in_order(theirs)
    for index in range(SLOTS):
        meta_out[index] = order_theirs[index]

    def remote(source, landing, sent, received, device):
        return pltpu.make_async_remote_copy(
            src_ref=source,
            dst_ref=landing,
            send_sem=sent,
            recv_sem=received,
            device_id=device,
            device_id_type=MESH,
        )

    def swap(index):
        return remote(swap_out.at[index], swap_in.at[index], swap_send.at[index], swap_recv.at[index], partner)

    def returned(region, index):
        return remote(
            fresh[1][region].at[index], back.at[index], back_send.at[index], back_recv.at[index], partner
        )

    meta = remote(meta_out, meta_in, meta_sem.at[0], meta_sem.at[1], partner)

    def landing_of(region, name):
        return 1 - region if name in (OUT_Z, IN_Z) else region

    def halo(step, region, name, which, rows=slice(0, EDGE)):
        landing = landing_of(region, name)
        cut = pl.ds(rows.start, rows.stop - rows.start)
        return remote(
            held[step][region].at[name if which else DIAG, cut],
            held[step][landing].at[beside(name) + which, cut],
            halo_send.at[step, region, name, which],
            halo_recv.at[step, landing, name],
            target[region, name],
        )

    def up_first(which):
        source = held[0][1].at[OUT_Z if which else DIAG]
        return remote(source, up.at[which], halo_send.at[0, 1, OUT_Z, which], via_recv.at[which], relay_of)

    def up_first_on(which):
        landing = held[0][0].at[beside(OUT_Z) + which]
        return remote(up.at[which], landing, via_send.at[which], halo_recv.at[0, 0, OUT_Z], onward)

    tail = pl.ds(EDGE - RELAYED, RELAYED)

    def up_second():
        return remote(held[1][1].at[OUT_Z, tail], up_late, via_send.at[5], via_recv.at[2], relay_of)

    def up_second_on():
        landing = held[1][0].at[beside(OUT_Z) + 1, tail]
        return remote(up_late, landing, via_send.at[2], halo_recv.at[1, 0, OUT_Z], onward)

    def down_first(which):
        source = held[0][0].at[OUT_Z if which else DIAG]
        return remote(source, down.at[which], halo_send.at[0, 0, OUT_Z, which], via_recv.at[3 + which], behind)

    def down_first_on(which):
        landing = held[0][1].at[beside(OUT_Z) + which]
        return remote(down.at[which], landing, via_send.at[3 + which], halo_recv.at[0, 1, OUT_Z], relay_for)

    def down_second():
        return remote(held[1][0].at[OUT_Z], down_late, halo_send.at[1, 0, OUT_Z, 1], via_recv.at[5], relay_for)

    def down_second_on():
        landing = held[1][1].at[beside(OUT_Z) + 1]
        return remote(down_late, landing, via_send.at[6], halo_recv.at[1, 1, OUT_Z], behind)

    def down_own():
        source = held[0][0].at[OUT_Z]
        return remote(source, down_mid, halo_send.at[0, 0, OUT_Z, 1], via_recv.at[6], relay_for)

    def down_own_on():
        landing = held[0][1].at[beside(OUT_Z) + 1]
        return remote(down_mid, landing, via_send.at[7], halo_recv.at[0, 1, OUT_Z], behind)

    def parts(step, region, name, which):
        whole = halo(step, region, name, which)
        if name != OUT_Z:
            return [(None, whole)]
        if step == 0:
            other = [down_first, up_first][region](which)
            if region == 0 and which == 1:
                return [(first_plane & own[1], other), (jnp.logical_not(first_plane), whole)]
            cut = first_plane if region == 0 else last_plane if which == 0 else last_plane & own[1]
            return [(cut, other), (jnp.logical_not(cut), whole)]
        if which == 0:
            return [(None, whole)]
        if region == 0:
            return [(first_plane, down_second()), (jnp.logical_not(first_plane), whole)]
        return [
            (last_plane, up_second()),
            (last_plane, halo(step, region, name, which, slice(0, EDGE - RELAYED))),
            (jnp.logical_not(last_plane), whole),
        ]

    def send(step, region, name, which):
        for condition, copy in parts(step, region, name, which):
            if condition is None:
                copy.start()
            else:
                pl.when(condition)(copy.start)

    for load in loads[4:]:
        load.wait()
    for index in range(SLOTS):
        chosen = loaded[1 - side, slot_theirs[index]]
        swap_out[index] = jnp.where(order_theirs[index] == NONE, nothing, chosen)
    for region in (0, 1):

        @pl.when(own[region])
        def _():
            for name in range(NONE):
                at = place(mine, name)
                chosen = loaded[side, jnp.minimum(at, SLOTS - 1)]
                held[0][region][name] = jnp.where(at == SLOTS, nothing, chosen)

    pl.semaphore_wait(barrier, jnp.where(first_plane, 7, jnp.where(last_plane, 8, 6)))
    pl.when(first_plane | last_plane)(lambda: greet(across))
    pl.when(first_plane)(lambda: greet(relay_for))
    pl.when(last_plane)(lambda: greet(relay_of))
    meta.start()
    at_jump = first_plane | last_plane
    edge_row = jnp.where(last_plane, 1, 0)

    def own_halos(region, which):
        send(0, region, OUT_X, which)
        send(0, region, OUT_Z, which)

    def own_inner(region):
        for name in (IN_X, IN_Z):
            for which in (0, 1):
                send(0, region, name, which)

    for region in (0, 1):

        @pl.when(own[region] & jnp.logical_not(at_jump & (edge_row != region)))
        def _():
            swap(0).start()
            own_halos(region, 0)
            swap(1).start()
            own_halos(region, 1)
            swap(2).start()
            own_inner(region)

        @pl.when(own[region] & at_jump & (edge_row != region))
        def _():
            own_halos(region, 0)
            own_halos(region, 1)
            own_inner(region)
            pl.semaphore_wait(turn, 1)
            for index in range(SLOTS):
                swap(index).start()

    @pl.when(at_jump & (core == edge_row))
    def _():
        swap(1).wait_send()
        pl.semaphore_signal(turn, 1, device_id=(sibling, col), device_id_type=MESH)

    meta.wait_recv()
    order_other = [meta_in[index] for index in range(SLOTS)]
    first, second, third = order_other
    for region in (0, 1):

        @pl.when(jnp.logical_not(own[region]))
        def _():
            swap(0).wait_recv()
            held[0][region][OUT_X] = jnp.where(first == OUT_X, swap_in[0], nothing)
            send(0, region, OUT_X, 1)
            swap(1).wait_recv()
            held[0][region][DIAG] = jnp.where(
                first == DIAG, swap_in[0], jnp.where(second == DIAG, swap_in[1], nothing)
            )
            for name in (OUT_X, OUT_Z, IN_X, IN_Z):
                send(0, region, name, 0)
            swap(2).wait_recv()
            for name in (OUT_Z, IN_Z, IN_X):
                at = place(order_other, name)
                chosen = swap_in[jnp.minimum(at, SLOTS - 1)]
                held[0][region][name] = jnp.where(at == SLOTS, nothing, chosen)
                send(0, region, name, 1)

    @pl.when(first_plane)
    def _():
        pl.semaphore_wait(barrier, 2)
        pl.when(own[0])(down_own().start)
        down_first(0).wait_recv()
        down_first_on(0).start()

    @pl.when(first_plane & own[1])
    def _():
        down_first(1).wait_recv()
        down_first_on(1).start()

    @pl.when(last_plane & own[1])
    def _():
        down_own().wait_recv()
        down_own_on().start()

    mine_first, mine_has = diagonal_first(order_mine)
    other_first, other_has = diagonal_first(order_other)
    layout = [
        (
            [jnp.where(own[region], a, b) for a, b in zip(mine_first, other_first)],
            (own[region] & mine_has) | (jnp.logical_not(own[region]) & other_has),
        )
        for region in (0, 1)
    ]

    def arrived(step, region):
        for name in BESIDE:
            pair = held[step][region].at[pl.ds(beside(name), 2)]
            pltpu.make_async_copy(pair, pair, halo_recv.at[step, region, name]).wait()

    def purify(step, region, done):
        names, has = layout[region]

        def at(index):
            return held[step][region][index]

        none = [name == NONE for name in names]
        diagonal = at(DIAG)
        left = [at(name) for name in names]
        right = at(jnp.where(has, DIAG, jnp.where(none[0], NONE, beside(names[0]))))
        over = [None] + [at(jnp.where(none[i], NONE, beside(names[i]))) for i in (1, 2)]
        towards = [None] + [
            at(jnp.where(none[i] | jnp.logical_not(has), NONE, beside(names[i]) + 1)) for i in (1, 2)
        ]
        square = [
            matmul(left[0], right) + matmul(left[1], towards[1]) + matmul(left[2], towards[2]),
            matmul(diagonal, left[1]) + matmul(left[1], over[1]),
            matmul(diagonal, left[2]) + matmul(left[2], over[2]),
        ]
        low = [s.astype(jnp.bfloat16) for s in square]
        centre = jnp.where(has, low[0], nothing)
        for index in range(SLOTS):
            if index == 0:
                cube = matmul(low[0], right) + matmul(low[1], towards[1]) + matmul(low[2], towards[2])
            else:
                cube = matmul(centre, left[index]) + matmul(low[index], over[index])
            fresh[step][region][index] = (3.0 * low[index].astype(jnp.float32) - 2.0 * cube).astype(jnp.bfloat16)
            done(index)

    def spread(region):
        for name in range(NONE):
            held[1][region][name] = fresh[0][region][place(layout[region][0], name)]
        for which in (0, 1):
            for name in (OUT_Z, OUT_X) if region else (OUT_X, OUT_Z):
                send(1, region, name, which)
        for name in (IN_X, IN_Z):
            for which in (0, 1):
                send(1, region, name, which)

    def give_back(region, index):
        pl.when(jnp.logical_not(own[region]))(returned(region, index).start)

    @pl.when(first_plane)
    def _():
        up_first(0).wait_recv()
        up_first_on(0).start()

    @pl.when(first_plane & own[0])
    def _():
        up_first(1).wait_recv()
        up_first_on(1).start()

    arrived(0, 1)
    purify(0, 1, lambda index: None)
    spread(1)

    arrived(0, 0)
    purify(0, 0, lambda index: None)
    spread(0)

    @pl.when(first_plane)
    def _():
        up_second().wait_recv()
        up_second_on().start()

    @pl.when(last_plane)
    def _():
        down_second().wait_recv()
        down_second_on().start()

    def finish(region):
        arrived(1, region)
        purify(1, region, functools.partial(give_back, region))

    pl.when(last_plane)(lambda: finish(0))
    finish(1)
    pl.when(jnp.logical_not(last_plane))(lambda: finish(0))

    def write(out, names, order, source):
        for slot in range(SLOTS):
            out[slot] = source[place(diagonal_first(order)[0], names[slot])]

    outs = (out_a, out_b)
    for which_side in (0, 1):
        for region in (0, 1):

            @pl.when((side == which_side) & own[region])
            def _():
                write(outs[which_side], mine, order_mine, fresh[1][region])

    for index in range(SLOTS):
        returned(0, index).wait_recv()
    for which_side in (0, 1):

        @pl.when(side == which_side)
        def _():
            write(outs[1 - which_side], theirs, order_theirs, back)

    meta.wait_send()
    for index in range(SLOTS):
        if index == 1:
            pl.when(jnp.logical_not(at_jump & (core == edge_row)))(swap(index).wait_send)
        else:
            swap(index).wait_send()
        returned(0, index).wait_send()
    for step in (0, 1):
        for region in (0, 1):
            for name in BESIDE:
                for which in (0, 1):
                    for condition, copy in parts(step, region, name, which):
                        if condition is None:
                            copy.wait_send()
                        else:
                            pl.when(condition)(copy.wait_send)

    pl.when(last_plane)(down_second_on().wait_send)

    @pl.when(first_plane)
    def _():
        up_second_on().wait_send()
        up_first_on(0).wait_send()
        pl.when(own[0])(up_first_on(1).wait_send)
        down_first_on(0).wait_send()
        pl.when(own[0])(down_own().wait_send)
        pl.when(own[1])(down_first_on(1).wait_send)

    pl.when(last_plane & own[1])(down_own_on().wait_send)


def per_device(dens_a, dens_b, codes_a, codes_b, counts_a, counts_b):
    stored = (SLOTS, EDGE, EDGE)
    shape = dens_a.shape
    in_vmem = pl.BlockSpec(memory_space=pltpu.VMEM)
    in_hbm = pl.BlockSpec(memory_space=pltpu.HBM)
    new_a, new_b = pl.pallas_call(
        kernel,
        out_shape=[pltpu.VMEM(stored, jnp.bfloat16)] * 2,
        in_specs=[in_hbm] * 6,
        out_specs=[in_vmem, in_vmem],
        scratch_shapes=[
            pltpu.SMEM((SLOTS,), jnp.int32),
            pltpu.SMEM((SLOTS,), jnp.int32),
            pltpu.SMEM((1,), jnp.int32),
            pltpu.SMEM((1,), jnp.int32),
            pltpu.VMEM((2, *stored), jnp.bfloat16),
            pltpu.VMEM(stored, jnp.bfloat16),
            pltpu.VMEM(stored, jnp.bfloat16),
            pltpu.SMEM((SLOTS,), jnp.int32),
            pltpu.SMEM((SLOTS,), jnp.int32),
            pltpu.VMEM((2, EDGE, EDGE), jnp.bfloat16),
            pltpu.VMEM((RELAYED, EDGE), jnp.bfloat16),
            pltpu.VMEM((2, EDGE, EDGE), jnp.bfloat16),
            pltpu.VMEM((EDGE, EDGE), jnp.bfloat16),
            pltpu.VMEM((EDGE, EDGE), jnp.bfloat16),
            *[pltpu.VMEM((HELD, EDGE, EDGE), jnp.bfloat16)] * 4,
            *[pltpu.VMEM((SLOTS + 1, EDGE, EDGE), jnp.bfloat16)] * 5,
            pltpu.SemaphoreType.DMA((6,)),
            pltpu.SemaphoreType.DMA((SLOTS,)),
            pltpu.SemaphoreType.DMA((SLOTS,)),
            pltpu.SemaphoreType.DMA((2,)),
            pltpu.SemaphoreType.DMA((2, 2, NONE, 2)),
            pltpu.SemaphoreType.DMA((2, 2, NONE)),
            pltpu.SemaphoreType.DMA((SLOTS,)),
            pltpu.SemaphoreType.DMA((SLOTS,)),
            pltpu.SemaphoreType.DMA((8,)),
            pltpu.SemaphoreType.DMA((7,)),
            pltpu.SemaphoreType.REGULAR,
        ],
        compiler_params=pltpu.CompilerParams(
            collective_id=0, has_side_effects=True, vmem_limit_bytes=60 * 2**20
        ),
        name="purify",
    )(
        dens_a.reshape(stored),
        dens_b.reshape(stored),
        codes_a.reshape(SLOTS),
        codes_b.reshape(SLOTS),
        counts_a.reshape(1),
        counts_b.reshape(1),
    )
    return new_a.reshape(shape), new_b.reshape(shape)


def solution(mesh):
    placed = (
        P("row", "col", None, None, None, None),
        P("row", "col", None, None, None, None),
        P("row", "col", None, None),
        P("row", "col", None, None),
        P("row", "col", None),
        P("row", "col", None),
    )
    return jax.shard_map(
        per_device,
        mesh=mesh,
        in_specs=placed,
        out_specs=(
            P("row", "col", None, None, None, None),
            P("row", "col", None, None, None, None),
        ),
        check_vma=False,
    )
```

```python
import functools

import jax
import jax.numpy as jnp
from jax import lax
from jax.experimental import pallas as pl
from jax.experimental.pallas import tpu as pltpu
from jax.sharding import PartitionSpec as P

OUT_X, DIAG, OUT_Z, IN_X, IN_Z, NONE = range(6)
BESIDE = (OUT_X, OUT_Z, IN_X, IN_Z)
MESH = pl.DeviceIdType.MESH
EDGE = 256
SLOTS = 3
HELD = 16
RELAYED = 128


def beside(name):
    return NONE + 1 + 2 * name


def names_of(codes_ref, count_ref, row_bit, col_bit):
    names = []
    for slot in range(SLOTS):
        code = codes_ref[slot]
        vertical = jnp.where(code - 1 == row_bit, OUT_Z, IN_Z)
        lateral = jnp.where(code - 3 == col_bit, OUT_X, IN_X)
        name = jnp.where(code == 0, DIAG, jnp.where(code <= 2, vertical, lateral))
        names.append(jnp.where(slot < count_ref[0], name, NONE))
    return names


def in_order(names):
    a, b, c = (names[slot] * 4 + slot for slot in range(SLOTS))
    a, b = jnp.minimum(a, b), jnp.maximum(a, b)
    b, c = jnp.minimum(b, c), jnp.maximum(b, c)
    a, b = jnp.minimum(a, b), jnp.maximum(a, b)
    return [v // 4 for v in (a, b, c)], [v % 4 for v in (a, b, c)]


def diagonal_first(order):
    first, second, third = order
    has = (first == DIAG) | (second == DIAG)
    return [jnp.where(has, DIAG, first), jnp.where(second == DIAG, first, second), third], has


def place(names, wanted):
    at = jnp.int32(SLOTS)
    for index in reversed(range(SLOTS)):
        at = jnp.where(names[index] == wanted, index, at)
    return at


def matmul(x, y):
    return jnp.dot(x, y, preferred_element_type=jnp.float32)


def kernel(
    dens_a, dens_b, codes_a_hbm, codes_b_hbm, count_a_hbm, count_b_hbm, out_a, out_b,
    codes_a, codes_b, count_a, count_b, loaded, swap_out, swap_in, meta_out, meta_in, up, up_late, down, down_late, down_mid,
    held_00, held_01, held_10, held_11, fresh_00, fresh_01, fresh_10, fresh_11, back,
    load_sem, swap_send, swap_recv, meta_sem, halo_send, halo_recv, back_send, back_recv, via_send, via_recv, turn,
):
    held = ((held_00, held_01), (held_10, held_11))
    fresh = ((fresh_00, fresh_01), (fresh_10, fresh_11))
    row, col = lax.axis_index("row"), lax.axis_index("col")
    core, side = lax.rem(row, 2), lax.rem(col, 2)
    own = [core == region for region in (0, 1)]
    depth = lax.rem(row // 2, 8)
    first_plane, last_plane = depth == 0, depth == 7
    sibling = row + 1 - 2 * core
    step_col = 2 * side - 1

    def wrapped(r, c):
        return (lax.rem(r + 64, 64), lax.rem(c + 8, 8))

    partner = (sibling, col - step_col)
    target = {}
    for region in (0, 1):
        target[region, OUT_X] = wrapped(sibling, col + jnp.where(own[region], 2, -2) * step_col)
        target[region, OUT_Z] = wrapped(sibling + 4 * region - 2, col)
        target[region, IN_X] = target[region, IN_Z] = (sibling, col)
    across = tuple(jnp.where(first_plane, a, b) for a, b in zip(target[0, OUT_Z], target[1, OUT_Z]))
    onward, behind = wrapped(row + 16, col), wrapped(row - 16, col)
    relay_of, relay_for = wrapped(sibling - 14, col), wrapped(sibling + 14, col)

    loads = [
        pltpu.make_async_copy(source, home, load_sem.at[index])
        for index, (source, home) in enumerate(
            (
                (codes_a_hbm, codes_a),
                (codes_b_hbm, codes_b),
                (count_a_hbm, count_a),
                (count_b_hbm, count_b),
                (dens_a, loaded.at[0]),
                (dens_b, loaded.at[1]),
            )
        )
    ]
    for load in loads:
        load.start()
    barrier = pltpu.get_barrier_semaphore()

    def greet(device):
        pl.semaphore_signal(barrier, 1, device_id=device, device_id_type=MESH)

    for device in (partner, (sibling, col), target[0, OUT_X], target[1, OUT_X]):
        greet(device)
    pl.when(jnp.logical_not(first_plane))(lambda: greet(target[0, OUT_Z]))
    pl.when(jnp.logical_not(last_plane))(lambda: greet(target[1, OUT_Z]))

    pl.when(first_plane | last_plane)(lambda: greet(onward))
    pl.when(first_plane)(lambda: greet(behind))

    nothing = jnp.zeros((EDGE, EDGE), jnp.bfloat16)
    for region in (0, 1):
        for step in (0, 1):
            held[step][region][NONE] = nothing
            fresh[step][region][SLOTS] = nothing
    back[SLOTS] = nothing

    for load in loads[:4]:
        load.wait()
    names_a = names_of(codes_a, count_a, core, side)
    names_b = names_of(codes_b, count_b, core, side)
    mine = [jnp.where(side == 0, a, b) for a, b in zip(names_a, names_b)]
    theirs = [jnp.where(side == 0, b, a) for a, b in zip(names_a, names_b)]
    order_mine, _ = in_order(mine)
    order_theirs, slot_theirs = in_order(theirs)
    for index in range(SLOTS):
        meta_out[index] = order_theirs[index]

    def remote(source, landing, sent, received, device):
        return pltpu.make_async_remote_copy(
            src_ref=source,
            dst_ref=landing,
            send_sem=sent,
            recv_sem=received,
            device_id=device,
            device_id_type=MESH,
        )

    def swap(index):
        return remote(swap_out.at[index], swap_in.at[index], swap_send.at[index], swap_recv.at[index], partner)

    def returned(region, index):
        return remote(
            fresh[1][region].at[index], back.at[index], back_send.at[index], back_recv.at[index], partner
        )

    meta = remote(meta_out, meta_in, meta_sem.at[0], meta_sem.at[1], partner)

    def landing_of(region, name):
        return 1 - region if name in (OUT_Z, IN_Z) else region

    def halo(step, region, name, which, rows=slice(0, EDGE)):
        landing = landing_of(region, name)
        cut = pl.ds(rows.start, rows.stop - rows.start)
        return remote(
            held[step][region].at[name if which else DIAG, cut],
            held[step][landing].at[beside(name) + which, cut],
            halo_send.at[step, region, name, which],
            halo_recv.at[step, landing, name],
            target[region, name],
        )

    def up_first(which):
        source = held[0][1].at[OUT_Z if which else DIAG]
        return remote(source, up.at[which], halo_send.at[0, 1, OUT_Z, which], via_recv.at[which], relay_of)

    def up_first_on(which):
        landing = held[0][0].at[beside(OUT_Z) + which]
        return remote(up.at[which], landing, via_send.at[which], halo_recv.at[0, 0, OUT_Z], onward)

    tail = pl.ds(EDGE - RELAYED, RELAYED)

    def up_second():
        return remote(held[1][1].at[OUT_Z, tail], up_late, via_send.at[5], via_recv.at[2], relay_of)

    def up_second_on():
        landing = held[1][0].at[beside(OUT_Z) + 1, tail]
        return remote(up_late, landing, via_send.at[2], halo_recv.at[1, 0, OUT_Z], onward)

    def down_first(which):
        source = held[0][0].at[OUT_Z if which else DIAG]
        return remote(source, down.at[which], halo_send.at[0, 0, OUT_Z, which], via_recv.at[3 + which], behind)

    def down_first_on(which):
        landing = held[0][1].at[beside(OUT_Z) + which]
        return remote(down.at[which], landing, via_send.at[3 + which], halo_recv.at[0, 1, OUT_Z], relay_for)

    def down_second():
        return remote(held[1][0].at[OUT_Z], down_late, halo_send.at[1, 0, OUT_Z, 1], via_recv.at[5], relay_for)

    def down_second_on():
        landing = held[1][1].at[beside(OUT_Z) + 1]
        return remote(down_late, landing, via_send.at[6], halo_recv.at[1, 1, OUT_Z], behind)

    def down_own():
        source = held[0][0].at[OUT_Z]
        return remote(source, down_mid, halo_send.at[0, 0, OUT_Z, 1], via_recv.at[6], relay_for)

    def down_own_on():
        landing = held[0][1].at[beside(OUT_Z) + 1]
        return remote(down_mid, landing, via_send.at[7], halo_recv.at[0, 1, OUT_Z], behind)

    def parts(step, region, name, which):
        whole = halo(step, region, name, which)
        if name != OUT_Z:
            return [(None, whole)]
        if step == 0:
            other = [down_first, up_first][region](which)
            if region == 0 and which == 1:
                return [(first_plane & own[1], other), (jnp.logical_not(first_plane), whole)]
            cut = first_plane if region == 0 else last_plane if which == 0 else last_plane & own[1]
            return [(cut, other), (jnp.logical_not(cut), whole)]
        if which == 0:
            return [(None, whole)]
        if region == 0:
            return [(first_plane, down_second()), (jnp.logical_not(first_plane), whole)]
        return [
            (last_plane, up_second()),
            (last_plane, halo(step, region, name, which, slice(0, EDGE - RELAYED))),
            (jnp.logical_not(last_plane), whole),
        ]

    def send(step, region, name, which):
        for condition, copy in parts(step, region, name, which):
            if condition is None:
                copy.start()
            else:
                pl.when(condition)(copy.start)

    for load in loads[4:]:
        load.wait()
    for index in range(SLOTS):
        chosen = loaded[1 - side, slot_theirs[index]]
        swap_out[index] = jnp.where(order_theirs[index] == NONE, nothing, chosen)
    for region in (0, 1):

        @pl.when(own[region])
        def _():
            for name in range(NONE):
                at = place(mine, name)
                chosen = loaded[side, jnp.minimum(at, SLOTS - 1)]
                held[0][region][name] = jnp.where(at == SLOTS, nothing, chosen)

    pl.semaphore_wait(barrier, jnp.where(first_plane, 7, jnp.where(last_plane, 8, 6)))
    pl.when(first_plane | last_plane)(lambda: greet(across))
    pl.when(first_plane)(lambda: greet(relay_for))
    pl.when(last_plane)(lambda: greet(relay_of))
    meta.start()
    at_jump = first_plane | last_plane
    edge_row = jnp.where(last_plane, 1, 0)

    def own_halos(region, which):
        send(0, region, OUT_X, which)
        send(0, region, OUT_Z, which)

    def own_inner(region):
        for name in (IN_X, IN_Z):
            for which in (0, 1):
                send(0, region, name, which)

    for region in (0, 1):

        @pl.when(own[region] & jnp.logical_not(at_jump & (edge_row != region)))
        def _():
            swap(0).start()
            own_halos(region, 0)
            swap(1).start()
            own_halos(region, 1)
            swap(2).start()
            own_inner(region)

        @pl.when(own[region] & at_jump & (edge_row != region))
        def _():
            own_halos(region, 0)
            own_halos(region, 1)
            own_inner(region)
            pl.semaphore_wait(turn, 1)
            for index in range(SLOTS):
                swap(index).start()

    @pl.when(at_jump & (core == edge_row))
    def _():
        swap(1).wait_send()
        pl.semaphore_signal(turn, 1, device_id=(sibling, col), device_id_type=MESH)

    meta.wait_recv()
    order_other = [meta_in[index] for index in range(SLOTS)]
    first, second, third = order_other
    for region in (0, 1):

        @pl.when(jnp.logical_not(own[region]))
        def _():
            swap(0).wait_recv()
            held[0][region][OUT_X] = jnp.where(first == OUT_X, swap_in[0], nothing)
            send(0, region, OUT_X, 1)
            swap(1).wait_recv()
            held[0][region][DIAG] = jnp.where(
                first == DIAG, swap_in[0], jnp.where(second == DIAG, swap_in[1], nothing)
            )
            for name in (OUT_X, OUT_Z, IN_X, IN_Z):
                send(0, region, name, 0)
            swap(2).wait_recv()
            for name in (OUT_Z, IN_Z, IN_X):
                at = place(order_other, name)
                chosen = swap_in[jnp.minimum(at, SLOTS - 1)]
                held[0][region][name] = jnp.where(at == SLOTS, nothing, chosen)
                send(0, region, name, 1)

    @pl.when(first_plane)
    def _():
        pl.semaphore_wait(barrier, 2)
        pl.when(own[0])(down_own().start)
        down_first(0).wait_recv()
        down_first_on(0).start()

    @pl.when(first_plane & own[1])
    def _():
        down_first(1).wait_recv()
        down_first_on(1).start()

    @pl.when(last_plane & own[1])
    def _():
        down_own().wait_recv()
        down_own_on().start()

    mine_first, mine_has = diagonal_first(order_mine)
    other_first, other_has = diagonal_first(order_other)
    layout = [
        (
            [jnp.where(own[region], a, b) for a, b in zip(mine_first, other_first)],
            (own[region] & mine_has) | (jnp.logical_not(own[region]) & other_has),
        )
        for region in (0, 1)
    ]

    def arrived(step, region):
        for name in BESIDE:
            pair = held[step][region].at[pl.ds(beside(name), 2)]
            pltpu.make_async_copy(pair, pair, halo_recv.at[step, region, name]).wait()

    def purify(step, region, done):
        names, has = layout[region]

        def at(index):
            return held[step][region][index]

        none = [name == NONE for name in names]
        diagonal = at(DIAG)
        left = [at(name) for name in names]
        right = at(jnp.where(has, DIAG, jnp.where(none[0], NONE, beside(names[0]))))
        over = [None] + [at(jnp.where(none[i], NONE, beside(names[i]))) for i in (1, 2)]
        towards = [None] + [
            at(jnp.where(none[i] | jnp.logical_not(has), NONE, beside(names[i]) + 1)) for i in (1, 2)
        ]
        square = [
            matmul(left[0], right) + matmul(left[1], towards[1]) + matmul(left[2], towards[2]),
            matmul(diagonal, left[1]) + matmul(left[1], over[1]),
            matmul(diagonal, left[2]) + matmul(left[2], over[2]),
        ]
        low = [s.astype(jnp.bfloat16) for s in square]
        centre = jnp.where(has, low[0], nothing)
        for index in range(SLOTS):
            if index == 0:
                cube = matmul(low[0], right) + matmul(low[1], towards[1]) + matmul(low[2], towards[2])
            else:
                cube = matmul(centre, left[index]) + matmul(low[index], over[index])
            fresh[step][region][index] = (3.0 * low[index].astype(jnp.float32) - 2.0 * cube).astype(jnp.bfloat16)
            done(index)

    def spread(region):
        for name in range(NONE):
            held[1][region][name] = fresh[0][region][place(layout[region][0], name)]
        for which in (1, 0) if region else (0, 1):
            for name in (OUT_Z, OUT_X) if region else (OUT_X, OUT_Z):
                send(1, region, name, which)
        for name in (IN_X, IN_Z):
            for which in (0, 1):
                send(1, region, name, which)

    def give_back(region, index):
        pl.when(jnp.logical_not(own[region]))(returned(region, index).start)

    @pl.when(first_plane)
    def _():
        up_first(0).wait_recv()
        up_first_on(0).start()

    @pl.when(first_plane & own[0])
    def _():
        up_first(1).wait_recv()
        up_first_on(1).start()

    arrived(0, 1)
    purify(0, 1, lambda index: None)
    spread(1)

    arrived(0, 0)
    purify(0, 0, lambda index: None)
    spread(0)

    @pl.when(first_plane)
    def _():
        up_second().wait_recv()
        up_second_on().start()

    @pl.when(last_plane)
    def _():
        down_second().wait_recv()
        down_second_on().start()

    def finish(region):
        arrived(1, region)
        purify(1, region, functools.partial(give_back, region))

    pl.when(last_plane)(lambda: finish(0))
    finish(1)
    pl.when(jnp.logical_not(last_plane))(lambda: finish(0))

    def write(out, names, order, source):
        for slot in range(SLOTS):
            out[slot] = source[place(diagonal_first(order)[0], names[slot])]

    outs = (out_a, out_b)
    for which_side in (0, 1):
        for region in (0, 1):

            @pl.when((side == which_side) & own[region])
            def _():
                write(outs[which_side], mine, order_mine, fresh[1][region])

    for index in range(SLOTS):
        returned(0, index).wait_recv()
    for which_side in (0, 1):

        @pl.when(side == which_side)
        def _():
            write(outs[1 - which_side], theirs, order_theirs, back)

    meta.wait_send()
    for index in range(SLOTS):
        if index == 1:
            pl.when(jnp.logical_not(at_jump & (core == edge_row)))(swap(index).wait_send)
        else:
            swap(index).wait_send()
        returned(0, index).wait_send()
    for step in (0, 1):
        for region in (0, 1):
            for name in BESIDE:
                for which in (0, 1):
                    for condition, copy in parts(step, region, name, which):
                        if condition is None:
                            copy.wait_send()
                        else:
                            pl.when(condition)(copy.wait_send)

    pl.when(last_plane)(down_second_on().wait_send)

    @pl.when(first_plane)
    def _():
        up_second_on().wait_send()
        up_first_on(0).wait_send()
        pl.when(own[0])(up_first_on(1).wait_send)
        down_first_on(0).wait_send()
        pl.when(own[0])(down_own().wait_send)
        pl.when(own[1])(down_first_on(1).wait_send)

    pl.when(last_plane & own[1])(down_own_on().wait_send)


def per_device(dens_a, dens_b, codes_a, codes_b, counts_a, counts_b):
    stored = (SLOTS, EDGE, EDGE)
    shape = dens_a.shape
    in_vmem = pl.BlockSpec(memory_space=pltpu.VMEM)
    in_hbm = pl.BlockSpec(memory_space=pltpu.HBM)
    new_a, new_b = pl.pallas_call(
        kernel,
        out_shape=[pltpu.VMEM(stored, jnp.bfloat16)] * 2,
        in_specs=[in_hbm] * 6,
        out_specs=[in_vmem, in_vmem],
        scratch_shapes=[
            pltpu.SMEM((SLOTS,), jnp.int32),
            pltpu.SMEM((SLOTS,), jnp.int32),
            pltpu.SMEM((1,), jnp.int32),
            pltpu.SMEM((1,), jnp.int32),
            pltpu.VMEM((2, *stored), jnp.bfloat16),
            pltpu.VMEM(stored, jnp.bfloat16),
            pltpu.VMEM(stored, jnp.bfloat16),
            pltpu.SMEM((SLOTS,), jnp.int32),
            pltpu.SMEM((SLOTS,), jnp.int32),
            pltpu.VMEM((2, EDGE, EDGE), jnp.bfloat16),
            pltpu.VMEM((RELAYED, EDGE), jnp.bfloat16),
            pltpu.VMEM((2, EDGE, EDGE), jnp.bfloat16),
            pltpu.VMEM((EDGE, EDGE), jnp.bfloat16),
            pltpu.VMEM((EDGE, EDGE), jnp.bfloat16),
            *[pltpu.VMEM((HELD, EDGE, EDGE), jnp.bfloat16)] * 4,
            *[pltpu.VMEM((SLOTS + 1, EDGE, EDGE), jnp.bfloat16)] * 5,
            pltpu.SemaphoreType.DMA((6,)),
            pltpu.SemaphoreType.DMA((SLOTS,)),
            pltpu.SemaphoreType.DMA((SLOTS,)),
            pltpu.SemaphoreType.DMA((2,)),
            pltpu.SemaphoreType.DMA((2, 2, NONE, 2)),
            pltpu.SemaphoreType.DMA((2, 2, NONE)),
            pltpu.SemaphoreType.DMA((SLOTS,)),
            pltpu.SemaphoreType.DMA((SLOTS,)),
            pltpu.SemaphoreType.DMA((8,)),
            pltpu.SemaphoreType.DMA((7,)),
            pltpu.SemaphoreType.REGULAR,
        ],
        compiler_params=pltpu.CompilerParams(
            collective_id=0, has_side_effects=True, vmem_limit_bytes=60 * 2**20
        ),
        name="purify",
    )(
        dens_a.reshape(stored),
        dens_b.reshape(stored),
        codes_a.reshape(SLOTS),
        codes_b.reshape(SLOTS),
        counts_a.reshape(1),
        counts_b.reshape(1),
    )
    return new_a.reshape(shape), new_b.reshape(shape)


def solution(mesh):
    placed = (
        P("row", "col", None, None, None, None),
        P("row", "col", None, None, None, None),
        P("row", "col", None, None),
        P("row", "col", None, None),
        P("row", "col", None),
        P("row", "col", None),
    )
    return jax.shard_map(
        per_device,
        mesh=mesh,
        in_specs=placed,
        out_specs=(
            P("row", "col", None, None, None, None),
            P("row", "col", None, None, None, None),
        ),
        check_vma=False,
    )
```
